128 devices in a mesh: dp: 64 (over x_hi, z, y, core), tensor: 2 (over x_lo).
Axes of the slice: x: 4 (x_hi: 2, x_lo: 2; x = x_hi * 2 + x_lo), y: 4, z: 4, core: 2. Of those that a mesh axis runs over, the one named last changes fastest.
Arguments:
- tokens: bfloat16 [16384, 2048], P(('dp', 'tensor')), may hold values from -6 to 6
- piece_starts: int32 [64, 2], P('dp'), may hold values from 0 to 192, as said below
- ln1_gain: float32 [2048], P(('dp', 'tensor')), may hold values from 0.5 to 1.5
- ln1_bias: float32 [2048], P(('dp', 'tensor')), may hold values from -0.3 to 0.3
- qkv_weight: bfloat16 [2048, 6144], P('dp', 'tensor'), may hold values from -0.125 to 0.125
- qkv_bias: float32 [6144], P(('dp', 'tensor')), may hold values from -0.3 to 0.3
- out_weight: bfloat16 [2048, 2048], P('dp', 'tensor'), may hold values from -0.375 to 0.375
- out_bias: float32 [2048], P(('dp', 'tensor')), may hold values from -0.3 to 0.3
- ln2_gain: float32 [2048], P(('dp', 'tensor')), may hold values from 0.5 to 1.5
- ln2_bias: float32 [2048], P(('dp', 'tensor')), may hold values from -0.3 to 0.3
- up_weight: bfloat16 [2048, 8192], P('dp', 'tensor'), may hold values from -0.125 to 0.125
- up_bias: float32 [8192], P(('dp', 'tensor')), may hold values from -0.3 to 0.3
- down_weight: bfloat16 [2048, 8192], P('dp', 'tensor'), may hold values from -0.0625 to 0.0625
- down_bias: float32 [2048], P(('dp', 'tensor')), may hold values from -0.3 to 0.3
- cotangent: bfloat16 [16384, 2048], P(('dp', 'tensor')), may hold values from -6 to 6
Outputs:
- layer_out: bfloat16 [16384, 2048], P(('dp', 'tensor'))
- grad_tokens: float32 [16384, 2048], P(('dp', 'tensor'))
- grad_ln1_gain: float32 [2048], P(('dp', 'tensor'))
- grad_ln1_bias: float32 [2048], P(('dp', 'tensor'))
- grad_qkv_weight: float32 [2048, 6144], P('dp', 'tensor')
- grad_qkv_bias: float32 [6144], P(('dp', 'tensor'))
- grad_out_weight: float32 [2048, 2048], P('dp', 'tensor')
- grad_out_bias: float32 [2048], P(('dp', 'tensor'))
- grad_ln2_gain: float32 [2048], P(('dp', 'tensor'))
- grad_ln2_bias: float32 [2048], P(('dp', 'tensor'))
- grad_up_weight: float32 [2048, 8192], P('dp', 'tensor')
- grad_up_bias: float32 [8192], P(('dp', 'tensor'))
- grad_down_weight: float32 [2048, 8192], P('dp', 'tensor')
- grad_down_bias: float32 [2048], P(('dp', 'tensor'))
The draws below stay inside these ranges and needn't reach their ends.
Inputs may be any that keep to these rules, and one draw needn't show every extreme that they name: `piece_starts`: row b holds the first positions of the 2 picture pieces of sequence b in increasing order; each piece covers 64 positions, pieces do not intersect and end inside the sequence.
All inputs are finite; a program needn't handle non-finite values.
Results may differ from the reference program's by a relative error of at most 0.017.
Values may be sent and summed in bfloat16 or wider, within the bound.
No kernel may reach another device: no remote copies, remote signals or barrier semaphores. Data moves between devices by JAX's collectives and lax.ppermute only.
A program may use at most 384 MiB of HBM per device.

```python
import math
import jax
import jax.numpy as jnp
from jax import lax

D = 2048
H = 16
HD = 128
FF = 8192
PIECE = 64
PIECES = 2
SEQ = 256
SEQS = 64
TOKENS = 16384


def draw_piece_starts(key, part):
    key = jax.random.fold_in(key, 7)
    text_len = SEQ - PIECES * PIECE
    cut_key, pick_key = jax.random.split(key)
    cut_points = jnp.sort(jax.random.randint(cut_key, (SEQS, PIECES), 0, text_len + 1, dtype=jnp.int32), axis=1)
    chosen = jax.random.randint(pick_key, (), 0, SEQS, dtype=jnp.int32)
    piece_order = jnp.arange(PIECES, dtype=jnp.int32)
    spread_row = jnp.where(piece_order[None, :] == 0, 0, jnp.where(piece_order[None, :] == PIECES - 1, text_len, cut_points))
    row_ids = jnp.arange(SEQS, dtype=jnp.int32)[:, None]
    cut_points = jnp.where(row_ids == chosen, spread_row, cut_points)
    return (cut_points + piece_order[None, :] * PIECE).astype(jnp.int32)


def steps_of(own_key, extent, shards, least, top_value):
    factor_of = 1.0
    for axis_at, blocks in shards:
        draws = jax.random.uniform(jax.random.fold_in(jax.random.fold_in(own_key, 6), axis_at), (blocks,), jnp.float32, least / len(shards), top_value / len(shards))
        factor_of = factor_of * jnp.repeat(jnp.exp(draws), extent[axis_at] // blocks).reshape((-1,) + (1,) * (len(extent) - 1 - axis_at))
    return factor_of


def noise(own_key, shape, deviation, reach, pieces=(), held_as=jnp.bfloat16):
    values = deviation * jax.random.normal(own_key, shape, jnp.float32)
    if pieces:
        values = values * steps_of(own_key, shape, pieces, -0.22, 0.18)
    return jnp.clip(values, -reach, reach).astype(held_as)


def setup_inputs(seed: int = 0) -> dict:
    key_list = jax.random.split(jax.random.key(seed), 16)
    return {
        "tokens": noise(key_list[0], (TOKENS, D), 1.0, 6.0, ((0, 128),)),
        "piece_starts": draw_piece_starts(jax.random.fold_in(key_list[15], 71), 0),
        "ln1_gain": jnp.clip(1.0 + 0.1 * jax.random.normal(key_list[2], (D,), jnp.float32), 0.5, 1.5),
        "ln1_bias": jnp.clip(jax.random.uniform(key_list[3], (D,), jnp.float32, -0.3, 0.3) * steps_of(key_list[3], (D,), ((0, 128),), -0.4, 0.0), -0.3, 0.3),
        "qkv_weight": noise(key_list[4], (D, 3 * D), D ** -0.5, 0.125, ((0, 64), (1, 2))),
        "qkv_bias": jnp.clip(jax.random.uniform(key_list[5], (3 * D,), jnp.float32, -0.3, 0.3) * steps_of(key_list[5], (3 * D,), ((0, 128),), -0.4, 0.0), -0.3, 0.3),
        "out_weight": noise(key_list[6], (D, D), (D // 8) ** -0.5, 0.375, ((0, 64), (1, 2))),
        "out_bias": jnp.clip(jax.random.uniform(key_list[7], (D,), jnp.float32, -0.3, 0.3) * steps_of(key_list[7], (D,), ((0, 128),), -0.4, 0.0), -0.3, 0.3),
        "ln2_gain": jnp.clip(1.0 + 0.1 * jax.random.normal(key_list[8], (D,), jnp.float32), 0.5, 1.5),
        "ln2_bias": jnp.clip(jax.random.uniform(key_list[9], (D,), jnp.float32, -0.3, 0.3) * steps_of(key_list[9], (D,), ((0, 128),), -0.4, 0.0), -0.3, 0.3),
        "up_weight": noise(key_list[10], (D, FF), D ** -0.5, 0.125, ((0, 64), (1, 2))),
        "up_bias": jnp.clip(jax.random.uniform(key_list[11], (FF,), jnp.float32, -0.3, 0.3) * steps_of(key_list[11], (FF,), ((0, 128),), -0.4, 0.0), -0.3, 0.3),
        "down_weight": noise(key_list[12], (D, FF), FF ** -0.5, 0.0625, ((0, 64), (1, 2))),
        "down_bias": jnp.clip(jax.random.uniform(key_list[13], (D,), jnp.float32, -0.3, 0.3) * steps_of(key_list[13], (D,), ((0, 128),), -0.4, 0.0), -0.3, 0.3),
        "cotangent": noise(key_list[14], (TOKENS, D), 1.0, 6.0, ((0, 128),)),
    }


@jax.custom_vjp
def low(v):
    return lax.optimization_barrier(v.astype(jnp.bfloat16)).astype(jnp.float32)

@jax.custom_vjp
def low_back(v):
    return v

def low_keep(v):
    return (low(v), None)

def low_pass(kept, grad):
    return (grad,)

def back_keep(v):
    return (v, None)

def back_low(kept, grad):
    return (low(grad),)
low.defvjp(low_keep, low_pass)
low_back.defvjp(back_keep, back_low)
highest = lax.Precision.HIGHEST
epsilon = 1e-05
gelu_coef = math.sqrt(2.0 / math.pi)

def layer_norm(values, gain_vec, shift_vec):
    centre = values - lax.optimization_barrier(jnp.mean(values, axis=-1, keepdims=True))
    spread = lax.optimization_barrier(jnp.mean(centre * centre, axis=-1, keepdims=True))
    return centre * lax.rsqrt(spread + epsilon) * gain_vec + shift_vec

def gelu_tanh(values):
    return 0.5 * values * (1.0 + jnp.tanh(gelu_coef * (values + 0.044715 * values * values * values)))

def allowed_pairs(query_pos, key_pos, starts):
    inside_query = (query_pos[:, None] >= starts[None, :]) & (query_pos[:, None] < starts[None, :] + PIECE)
    inside_key = (key_pos[:, None] >= starts[None, :]) & (key_pos[:, None] < starts[None, :] + PIECE)
    shared = jnp.any(inside_query[:, None, :] & inside_key[None, :, :], axis=-1)
    return shared | (key_pos[None, :] <= query_pos[:, None])

def attend(queries, keys_all, values_all, starts):
    block_rows = min(512, SEQ)
    key_pos = jnp.arange(SEQ, dtype=jnp.int32)
    slopes = jnp.exp2(-8.0 * (jnp.arange(H, dtype=jnp.float32) + 1.0) / H)
    score_scale = 1.0 / math.sqrt(HD)

    def one_block(block_index):
        first_row = block_index * block_rows
        query_block = lax.dynamic_slice_in_dim(queries, first_row, block_rows, 1)
        query_pos = first_row + jnp.arange(block_rows, dtype=jnp.int32)
        raw_scores = low_back(jnp.einsum('gqhd,gkhd->ghqk', query_block, keys_all, precision=highest))
        distance = jnp.abs(query_pos[:, None] - key_pos[None, :]).astype(jnp.float32)
        scores = raw_scores * score_scale - slopes[None, :, None, None] * distance[None, None]
        allowed = jax.vmap(lambda one_start: allowed_pairs(query_pos, key_pos, one_start))(starts)
        scores = jnp.where(allowed[:, None], scores, -1e+30)
        row_max = lax.optimization_barrier(jnp.max(scores, axis=-1, keepdims=True))
        shifted_exp = jnp.exp(scores - row_max)
        attn_prob = low(shifted_exp / lax.optimization_barrier(jnp.sum(shifted_exp, axis=-1, keepdims=True)))
        return low_back(jnp.einsum('ghqk,gkhd->gqhd', attn_prob, values_all, precision=highest))
    blocks = lax.map(jax.checkpoint(one_block), jnp.arange(SEQ // block_rows, dtype=jnp.int32))
    return jnp.moveaxis(blocks, 0, 1).reshape(queries.shape)

def forward(starts, inputs, ln1_gain, ln1_bias, qkv_weight, qkv_bias, out_weight, out_bias, ln2_gain, ln2_bias, up_weight, up_bias, down_weight, down_bias):
    groups = inputs.shape[0]
    normed = low(layer_norm(inputs, ln1_gain, ln1_bias))
    joined_proj = low_back(jnp.einsum('gsi,io->gso', normed, qkv_weight, precision=highest))
    joined_proj = low(joined_proj + qkv_bias).reshape(groups, SEQ, H, 3, HD)
    mixed_heads = attend(joined_proj[:, :, :, 0], joined_proj[:, :, :, 1], joined_proj[:, :, :, 2], starts)
    mixed_heads = low(mixed_heads.reshape(groups, SEQ, D))
    branch = low_back(jnp.einsum('gsi,oi->gso', mixed_heads, out_weight, precision=highest)) + out_bias
    middle = inputs + branch
    normed_two = low(layer_norm(middle, ln2_gain, ln2_bias))
    hidden = low_back(jnp.einsum('gsi,if->gsf', normed_two, up_weight, precision=highest)) + up_bias
    active = low(gelu_tanh(hidden))
    branch_two = low_back(jnp.einsum('gsf,of->gso', active, down_weight, precision=highest)) + down_bias
    return middle + branch_two

def reference(tokens, piece_starts, ln1_gain, ln1_bias, qkv_weight, qkv_bias, out_weight, out_bias, ln2_gain, ln2_bias, up_weight, up_bias, down_weight, down_bias, cotangent):
    group_seqs = math.gcd(SEQS, max(1, 4096 // SEQ))
    step_count = SEQS // group_seqs
    params = tuple((param.astype(jnp.float32) for param in (ln1_gain, ln1_bias, qkv_weight, qkv_bias, out_weight, out_bias, ln2_gain, ln2_bias, up_weight, up_bias, down_weight, down_bias)))
    token_steps = tokens.astype(jnp.float32).reshape(step_count, group_seqs, SEQ, D)
    cot_steps = cotangent.astype(jnp.float32).reshape(step_count, group_seqs, SEQ, D)
    start_steps = piece_starts.reshape(step_count, group_seqs, PIECES)

    def one_step(totals, step_inputs):
        step_tokens, step_starts, step_cot = step_inputs
        result, pullback = jax.vjp(lambda moved, *weights: forward(step_starts, moved, *weights), step_tokens, *params)
        gradients = pullback(step_cot)
        totals = jax.tree.map(jnp.add, totals, tuple(gradients[1:]))
        return (totals, (result, gradients[0]))
    initial = tuple((jnp.zeros_like(param) for param in params))
    totals, (results, input_grads) = lax.scan(one_step, initial, (token_steps, start_steps, cot_steps))
    layer_out = results.reshape(TOKENS, D).astype(jnp.bfloat16)
    grad_tokens = input_grads.reshape(TOKENS, D)
    return (layer_out, grad_tokens, totals[0], totals[1], totals[2], totals[3], totals[4], totals[5], totals[6], totals[7], totals[8], totals[9], totals[10], totals[11])
```

```python
import functools
import math

import jax
import jax.numpy as jnp
from jax import lax
from jax.experimental import pallas as pl
from jax.experimental.pallas import tpu as pltpu
from jax.sharding import Mesh
from jax.sharding import PartitionSpec as P

H = 16
HD = 128
PIECE = 64
EPS = 1e-05
GELU_COEF = math.sqrt(2.0 / math.pi)
SCALE = 1.0 / math.sqrt(HD)

AXES = ("xh", "z", "y", "c", "t")
RING = ("xh", "t")
PLANE = ("z", "y")
BF16 = jnp.bfloat16
F32 = jnp.float32


def gelu_tanh(values):
    return (
        0.5 * values * (1.0 + jnp.tanh(GELU_COEF * (values + 0.044715 * values * values * values)))
    )


def gelu_slope(values):
    square = values * values
    inner = jnp.tanh(GELU_COEF * (values + 0.044715 * values * square))
    return 0.5 * (1.0 + inner) + 0.5 * values * (1.0 - inner * inner) * GELU_COEF * (
        1.0 + 3.0 * 0.044715 * square
    )


def contract_rows(left_side, right_side):
    return lax.dot_general(
        left_side, right_side, (((0,), (0,)), ((), ())), preferred_element_type=F32
    )


def contract_cols(left_side, right_side):
    return lax.dot_general(
        left_side, right_side, (((1,), (1,)), ((), ())), preferred_element_type=F32
    )


def swap_x(v, mask):
    return lax.ppermute(v, RING, [(i, i ^ mask) for i in range(4)])


def swap_c(v):
    return lax.ppermute(v, "c", [(0, 1), (1, 0)])


ANYWHERE = pl.BlockSpec(memory_space=pl.ANY)
VMEM = pl.BlockSpec(memory_space=pltpu.VMEM)
SCALARS = pl.BlockSpec(memory_space=pltpu.SMEM)


def small_call(kernel, outs, operands, *others, scalars=None):
    first = [] if scalars is None else [scalars]

    def run(*refs):
        used = len(first) + len(operands)
        kernel(*refs[:used], *refs[used + len(others) :])

    return pl.pallas_call(
        run,
        in_specs=[SCALARS] * len(first) + [VMEM] * len(operands) + [ANYWHERE] * len(others),
        out_specs=[VMEM] * len(outs),
        out_shape=[jax.ShapeDtypeStruct(shape, dtype) for shape, dtype in outs],
        compiler_params=pltpu.CompilerParams(vmem_limit_bytes=24 << 20),
        cost_estimate=pl.CostEstimate(flops=0, bytes_accessed=4 << 20, transcendentals=0),
    )(*first, *operands, *others)


def split_kernel(one_ref, three_ref, low_ref, high_ref):
    half = low_ref.shape[0]
    low_ref[...] = three_ref[:half]
    high_ref[...] = one_ref[half:]


def pile_kernel(*refs):
    *pieces, out_ref = refs
    at = 0
    for piece in pieces:
        rows = piece.shape[0]
        out_ref[at : at + rows] = piece[...]
        at += rows


def gather_start(v):
    return swap_x(v, 1), swap_x(v, 3)


def gather_split(came, *others):
    rows, width = came[0].shape
    return small_call(split_kernel, [((rows // 2, width), BF16)] * 2, came, *others)


def gather_onward(onward):
    return swap_x(onward[0], 1), swap_x(onward[1], 3)


def gather_finish(v, came, opposite, *others):
    rows, width = v.shape
    pieces = [v, came[0], *opposite, came[1]]
    (own,) = small_call(pile_kernel, [((4 * rows, width), BF16)], pieces, *others)
    return own, swap_c(own)


def gather_group(v):
    came = gather_start(v)
    return gather_finish(v, came, gather_onward(gather_split(came)))


def add_low(*values):
    return sum(v.astype(F32) for v in values).astype(BF16)


def swap_cores(far):
    near, beyond = far
    return swap_c(beyond), swap_c(near)


def ring_two_kernel(*refs):
    *ins, low_ref, high_ref = refs
    blocks = [
        add_low(own[256:384], beyond[:128]) for own, beyond in zip(ins[::2], ins[1::2], strict=True)
    ]
    whole = blocks[0] if len(blocks) == 1 else jnp.concatenate(blocks, axis=0)
    half = low_ref.shape[0]
    low_ref[...] = whole[:half]
    high_ref[...] = whole[half:]


def ring_two(sums, *others):
    ins = [v for own, _, beyond in sums for v in (own, beyond)]
    outs = [((64 * len(sums), 2048), BF16)] * 2
    low, high = small_call(ring_two_kernel, outs, ins, *others)
    return swap_x(low, 1), swap_x(high, 3)


def ring_next_kernel(*refs):
    *ins, add3_ref, add1_ref, s1_ref, s3_ref = refs
    one, three = [], []
    for own, near, beyond in zip(ins[::3], ins[1::3], ins[2::3], strict=True):
        one.append(own[128:256].astype(F32) + near[128:].astype(F32))
        three.append(own[384:].astype(F32) + beyond[128:].astype(F32))
    one = one[0] if len(one) == 1 else jnp.concatenate(one, axis=0)
    three = three[0] if len(three) == 1 else jnp.concatenate(three, axis=0)
    half = add3_ref.shape[0]
    s3_ref[:half] = (three[:half] + add3_ref[...].astype(F32)).astype(BF16)
    s3_ref[half:] = three[half:].astype(BF16)
    s1_ref[:half] = one[:half].astype(BF16)
    s1_ref[half:] = (one[half:] + add1_ref[...].astype(F32)).astype(BF16)


def ring_next(sums, came, *others):
    ins = [v for triple in sums for v in triple]
    outs = [((128 * len(sums), 2048), BF16)] * 2
    s1, s3 = small_call(ring_next_kernel, outs, [*ins, *came], *others)
    return swap_x(s1, 1), swap_x(s3, 3)


def axis_swap(v, axis, mask):
    return lax.ppermute(v, axis, [(i, i ^ mask) for i in range(4)])


def axis_next_kernel(*refs):
    for i in range(0, len(refs) // 2, 3):
        blocks, add3, add1 = refs[i : i + 3]
        one_ref, three_ref = refs[len(refs) * 3 // 5 + i // 3 * 2 :][:2]
        half = add3.shape[0]
        three_ref[:half] = add_low(blocks[3, :half], add3[...])
        three_ref[half:] = blocks[3, half:]
        one_ref[:half] = blocks[1, :half]
        one_ref[half:] = add_low(blocks[1, half:], add1[...])


def axis_next(axes, blocks, came, *others):
    a, b = blocks
    outs = [((a.shape[1], 512), BF16)] * 2 + [((b.shape[1], 512), BF16)] * 2
    one_a, three_a, one_b, three_b = small_call(
        axis_next_kernel, outs, [a, *came[:2], b, *came[2:]], *others
    )
    return (
        axis_swap(one_a, axes[0], 1),
        axis_swap(three_a, axes[0], 3),
        axis_swap(one_b, axes[1], 1),
        axis_swap(three_b, axes[1], 3),
    )


def axis_turn_kernel(a_ref, a1, a3, b_ref, b1, b3, oa_ref, ob_ref, al_ref, ah_ref, bl_ref, bh_ref):
    sum_a = add_low(a_ref[...], a1[...], a3[...]).reshape(4, 144, 512)
    sum_b = add_low(b_ref[...], b1[...], b3[...]).reshape(4, 128, 512)
    oa_ref[...] = sum_a
    ob_ref[...] = sum_b
    al_ref[...] = sum_a[2, :64]
    ah_ref[...] = sum_a[2, 64:]
    bl_ref[...] = sum_b[2, :64]
    bh_ref[...] = sum_b[2, 64:]


def axis_turn(a, b, came, *others):
    shapes = (4, 144, 512), (4, 128, 512), (64, 512), (80, 512), (64, 512), (64, 512)
    sum_a, sum_b, al, ah, bl, bh = small_call(
        axis_turn_kernel, [(v, BF16) for v in shapes], [a, *came[:2], b, *came[2:]], *others
    )
    sent = (
        axis_swap(al, "y", 1),
        axis_swap(ah, "y", 3),
        axis_swap(bl, "z", 1),
        axis_swap(bh, "z", 3),
    )
    return (sum_a, sum_b), sent


def exchange(own, near, far, cross):
    return (
        own,
        swap_c(near),
        lax.ppermute(far, "xh", [(0, 1), (1, 0)]),
        lax.ppermute(cross, ("xh", "c"), [(i, 3 - i) for i in range(4)]),
    )


def spread_kernel(me_ref, *refs):
    parts, outs = refs[:-4], refs[-4:]
    rows = outs[0].shape[0]
    for other, out_ref in enumerate(outs):
        quarter = me_ref[0] ^ other
        at = 0
        for part in parts:
            if part.shape[0] == 32:
                width = part.shape[1] // 4
                start = pl.multiple_of(quarter * width, 128)
                out_ref[:32, at : at + width] = part[:, pl.ds(start, width)]
                at += width
            else:
                out_ref[32:rows] = part[...]


def collect_kernel(me_ref, *refs):
    *came, out_ref = refs
    for other, part in enumerate(came):
        start = pl.multiple_of((me_ref[0] ^ other) * 32, 32)
        out_ref[pl.ds(start, 32)] = part[:32]
    if out_ref.shape[0] > 128:
        out_ref[128:] = add_low(*(part[32:] for part in came))


def spread_columns(me, parts, *others, extra=None):
    below = 0 if extra is None else 16
    width = sum(p.shape[1] for p in parts) // 4
    ins = list(parts) if extra is None else [*parts, extra]
    sent = small_call(spread_kernel, [((32 + below, width), BF16)] * 4, ins, *others, scalars=me)
    (rows,) = small_call(
        collect_kernel, [((128 + below, width), BF16)], exchange(*sent), scalars=me
    )
    return rows


def return_kernel(me_ref, a_ref, a1, a3, b_ref, b1, b3, second_ref, *outs):
    sum_a = add_low(a_ref[0], a1[...], a3[...])
    sum_b = add_low(b_ref[0], b1[...], b3[...])
    for at in range(4):
        rows = slice(at * 32, at * 32 + 32)

        for other, out_ref in enumerate(outs):

            @pl.when(me_ref[0] ^ other == at)
            def _():
                out_ref[:32, :512] = sum_a[rows]
                out_ref[:32, 512:1024] = sum_b[rows]
                out_ref[:32, 1024:] = second_ref[rows]

    for out_ref in outs:
        out_ref[32:, :512] = sum_a[128:]
        out_ref[32:, 512:] = jnp.zeros((16, 2560), BF16)


def place_kernel(me_ref, *refs):
    came, (qkv_ref, out_ref, up_ref, down_ref, sum_ref) = refs[:4], refs[4:]
    for other, part in enumerate(came):
        quarter = me_ref[0] ^ other
        for ref, first, width in (
            (qkv_ref, 0, 768),
            (out_ref, 768, 256),
            (up_ref, 1024, 1024),
            (down_ref, 2048, 1024),
        ):
            start = pl.multiple_of(quarter * width, 128)
            ref[:, pl.ds(start, width)] = part[:32, first : first + width].astype(F32)
    sum_ref[...] = sum(part[32:, :128].astype(F32) for part in came)


def two_pieces(v):
    high = lax.reduce_precision(v, 8, 7)
    return jnp.stack([high, v - high]).astype(BF16)


def small_block(vectors, joined_bias, unit_bias, starts, xh, c, t):
    flat = jnp.concatenate([*vectors, joined_bias, unit_bias])
    other = swap_x(flat, 1)
    pair = jnp.where(t == 0, jnp.stack([flat, other]), jnp.stack([other, flat]))
    pieces = two_pieces(pair)
    mine = (jnp.arange(4) == xh * 2 + c).astype(BF16)
    rows = pieces[:, :, :96].reshape(2, 2, 6, 16).transpose(2, 0, 1, 3).reshape(6, 2, 1, 32)
    rows = (rows * mine[:, None]).reshape(6, 256)
    joined = (pieces[:, :, 96:144].reshape(2, 1, 96) * mine[:, None]).reshape(2, 384)
    unit = (pieces[:, :, 144:].reshape(2, 1, 128) * mine[:, None]).reshape(2, 512)
    starts = (starts.astype(BF16) * mine[:, None]).reshape(1, 8)
    wide = lambda v: jnp.pad(v, ((0, 0), (0, 1024 - v.shape[1])))
    return jnp.concatenate(
        [wide(rows), wide(joined), wide(unit), wide(starts), jnp.zeros((5, 1024), BF16)], axis=0
    )


def small_vectors(gathered, quarter, t):
    rows = gathered[:, :8, :256].astype(F32)
    rows = (rows[:, :, :128] + rows[:, :, 128:]).transpose(1, 0, 2).reshape(8, 2048)
    take = lambda first, width: (
        lax.dynamic_slice(gathered, (quarter * 4, first, t * width), (4, 2, width))
        .astype(F32)
        .sum(axis=1)
        .reshape(1, 4 * width)
    )
    return rows, take(6, 192), take(8, 256)


def bias_rows(sums, quarter, t):
    w = sums.shape[1] // 16
    v = sums.reshape(4, 4, w // 16, 16).transpose(2, 0, 1, 3).reshape(w // 16, 4, 64)
    none = jnp.zeros_like(v)
    v = jnp.where(
        t == 0, jnp.concatenate([v, none], axis=2), jnp.concatenate([none, v], axis=2)
    ).reshape(w // 16, 512)
    return lax.dynamic_update_slice_in_dim(
        jnp.zeros((w // 16, 2048), F32), v, quarter * 512, 1
    )


def low_half(rows):
    return lax.broadcasted_iota(jnp.int32, (rows, 128), 1) < 64


def store_plane(ref, values):
    low = low_half(values.shape[0])
    for j in range(8):
        a = values[:, j * 128 : j * 128 + 128]
        b = values[:, 1024 + j * 128 : 1024 + j * 128 + 128]
        at = j * 256
        ref[:, at : at + 128] = jnp.where(low, a, pltpu.roll(b, 64, 1)).astype(ref.dtype)
        ref[:, at + 128 : at + 256] = jnp.where(low, pltpu.roll(a, 64, 1), b).astype(ref.dtype)


def natural(values):
    low = low_half(values.shape[0])
    first, second = [], []
    for j in range(8):
        a = values[:, j * 256 : j * 256 + 128]
        b = values[:, j * 256 + 128 : j * 256 + 256]
        first.append(jnp.where(low, a, pltpu.roll(b, 64, 1)))
        second.append(jnp.where(low, pltpu.roll(a, 64, 1), b))
    return jnp.concatenate(first + second, axis=1)


def total_of(refs):
    return natural(sum(r[...].astype(F32) for r in refs))


def row_stats(values):
    centre = values - jnp.mean(values, axis=-1, keepdims=True)
    spread = jnp.mean(centre * centre, axis=-1, keepdims=True)
    return centre, lax.rsqrt(spread + EPS)


def norm_back(values, gain, upstream):
    centre, scale = row_stats(values)
    vhat = centre * scale
    e = upstream * gain
    dv = scale * (
        e - jnp.mean(e, axis=-1, keepdims=True) - vhat * jnp.mean(e * vhat, axis=-1, keepdims=True)
    )
    return dv, vhat


def first_norm_kernel(x_ref, n_ref):
    centre, scale = row_stats(x_ref[...].reshape(256, 2048).astype(F32))
    store_plane(n_ref, centre * scale)


def middle_kernel(t0, t1, t2, t3, x_ref, small_ref, mid_ref, n_ref):
    small = natural(small_ref[...])
    middle = x_ref[...].astype(F32) + (total_of((t0, t1, t2, t3)) + small[2:3])
    mid_ref[...] = middle
    centre, scale = row_stats(middle)
    store_plane(n_ref, centre * scale * small[3:4] + small[4:5])


def second_back_kernel(t0, t1, t2, t3, mid_ref, cot_ref, small_ref, dh_ref, low_ref, sum_ref):
    small = natural(small_ref[...])
    upstream = total_of((t0, t1, t2, t3))
    dv, vhat = norm_back(mid_ref[...], small[3:4], upstream)
    final = cot_ref[...].astype(F32)
    dh = final + dv
    dh_ref[...] = dh
    store_plane(low_ref, dh)
    total = lambda v: jnp.sum(v, axis=0, keepdims=True)
    store_plane(
        sum_ref,
        jnp.concatenate(
            [total(dh), total(upstream * vhat), total(upstream), total(final), jnp.zeros((4, 2048), F32)],
            axis=0,
        ),
    )


def first_back_kernel(t0, t1, t2, t3, x_ref, dh_ref, small_ref, g_ref):
    small = natural(small_ref[...])
    dv, _ = norm_back(x_ref[...].astype(F32), small[0:1], total_of((t0, t1, t2, t3)))
    g_ref[...] = dh_ref[...] + dv


def output_kernel(t0, t1, t2, t3, mid_ref, small_ref, o_ref):
    small = natural(small_ref[...])
    o_ref[...] = (mid_ref[...] + (total_of((t0, t1, t2, t3)) + small[5:6])).astype(BF16)


def pack_kernel(x_ref, cot_ref, o_ref):
    o_ref[:128] = x_ref[...]
    store_plane(o_ref.at[128:], cot_ref[...].astype(F32))


PARAMS = pltpu.CompilerParams(vmem_limit_bytes=48 << 20)


def cost(flops, mebibytes):
    return pl.CostEstimate(flops=int(flops), bytes_accessed=int(mebibytes * 2**20), transcendentals=0)


def whole_call(kernel, outs, *operands):
    return pl.pallas_call(
        kernel, out_shape=outs, compiler_params=PARAMS, cost_estimate=cost(0, 4)
    )(*operands)


def row_block(width):
    return pl.BlockSpec((256, width), lambda i: (i, 0))


def whole(*shape):
    return pl.BlockSpec(shape, lambda i: (0,) * len(shape))


def halves(*block):
    tail = (0,) * (len(block) - 1)
    return [
        pl.BlockSpec(block, lambda i: (jnp.minimum(i, 1), *tail)),
        pl.BlockSpec(block, lambda i: (jnp.maximum(i - 2, 0), *tail)),
    ]


def pick(own_ref, other_ref):
    return jnp.where(pl.program_id(0) < 2, own_ref[...], other_ref[...])


def contract_both(own, other, right):
    half = right.shape[0] // 2
    return contract_rows(own, right[:half]) + contract_rows(other, right[half:])


def like(rows, dtype):
    return jax.ShapeDtypeStruct((rows, 2048), dtype)


def first_norm(packed):
    return pl.pallas_call(
        first_norm_kernel,
        grid=(2,),
        in_specs=[pl.BlockSpec((2, 1, 128, 2048), lambda i: (i, 0, 0, 0))],
        out_specs=pl.BlockSpec((256, 2048), lambda i: (i, 0)),
        out_shape=like(512, F32),
        compiler_params=PARAMS,
        cost_estimate=cost(0, 8),
    )(packed)


def up_grads_kernel(own_ref, other_ref, du_ref, out_ref, done_ref):
    done_ref[...] = jnp.zeros_like(done_ref)
    out_ref[...] = contract_both(own_ref[...], other_ref[...], du_ref[...]).astype(BF16)


def down_grads_kernel(_, own_ref, other_ref, a_ref, out_ref, done_ref):
    done_ref[...] = jnp.zeros_like(done_ref)
    own, other = own_ref[...].reshape(512, 512), other_ref[...].reshape(512, 512)
    out_ref[...] = contract_both(own, other, a_ref[...]).astype(BF16)


def up_grads(n, du):
    rows, width = du.shape
    return pl.pallas_call(
        up_grads_kernel,
        grid=(4,),
        in_specs=[pl.BlockSpec((512, 512), lambda i: (0, i))] * 2 + [whole(rows, width)],
        out_specs=[pl.BlockSpec((512, width), lambda i: (i, 0)), whole(8, 128)],
        out_shape=[
            jax.ShapeDtypeStruct((2048, 2 * width), BF16),
            jax.ShapeDtypeStruct((8, 128), F32),
        ],
        compiler_params=PARAMS,
        cost_estimate=cost(5e9, 10),
    )(*n, du)


def down_grads(left, packed, a):
    rows, width = a.shape
    return pl.pallas_call(
        down_grads_kernel,
        grid=(4,),
        in_specs=[ANYWHERE]
        + [pl.BlockSpec((4, 1, 128, 512), lambda i: (0, 1, 0, i))] * 2
        + [whole(rows, width)],
        out_specs=[pl.BlockSpec((512, width), lambda i: (i, 1)), whole(8, 128)],
        out_shape=[
            jax.ShapeDtypeStruct(left.shape, BF16),
            jax.ShapeDtypeStruct((8, 128), F32),
        ],
        input_output_aliases={0: 0},
        compiler_params=PARAMS,
        cost_estimate=cost(5e9, 10),
    )(left, *packed, a)


def first_grads_kernel(
    place_ref, n_ref, own_ref, other_ref, df_ref, o_ref, w_ref, total_ref, small_ref, sums_ref, a_ref, b_ref
):
    y = place_ref[1]
    joined = contract_rows(n_ref[...], df_ref[...])
    weight = w_ref[...].reshape(512, 768)
    weighted = joined * weight.astype(F32)
    weighted = sum(weighted[:, j * 128 : j * 128 + 128] for j in range(6))
    weighted = lax.dot_general(
        jnp.ones((8, 128), F32),
        weighted,
        (((1,), (1,)), ((), ())),
        preferred_element_type=F32,
        precision=lax.Precision.HIGHEST,
    )
    shift = contract_cols(total_ref[...].astype(BF16), weight)[0:1]
    gain = (weighted[0:1] - small_ref[1:2] * shift) / small_ref[0:1]
    rows = lax.broadcasted_iota(jnp.int32, (16, 512), 0)
    sums = jnp.where(rows == 4, gain, jnp.where(rows == 5, shift, sums_ref[...])).astype(BF16)
    joined = joined.astype(BF16)
    out = contract_both(own_ref[...], other_ref[...], o_ref[...]).astype(BF16)
    for i in range(4):
        rows = slice(i * 128, i * 128 + 128)
        a_ref[0, i ^ y, :128] = joined[rows, :512]
        a_ref[0, i ^ y, 128:, :128] = sums[:, rows]
        a_ref[0, i ^ y, 128:, 128:] = jnp.zeros((16, 384), BF16)
        b_ref[i ^ y, 0, :, :256] = joined[rows, 512:]
        b_ref[i ^ y, 0, :, 256:] = out[rows]


def first_grads_of(place, n, dh, df, o, first_all, total, small, sums):
    rows = n.shape[0]
    return pl.pallas_call(
        first_grads_kernel,
        grid_spec=pltpu.PrefetchScalarGridSpec(
            num_scalar_prefetch=1,
            grid=(4,),
            in_specs=[
                pl.BlockSpec((rows, 512), lambda i, p: (0, i)),
                pl.BlockSpec((512, 512), lambda i, p: (0, i)),
                pl.BlockSpec((512, 512), lambda i, p: (0, i)),
                pl.BlockSpec((rows, 768), lambda i, p: (0, 0)),
                pl.BlockSpec((rows, 256), lambda i, p: (0, 0)),
                pl.BlockSpec((4, 128, 768), lambda i, p: (i, 0, 0)),
                pl.BlockSpec((8, 768), lambda i, p: (0, 0)),
                pl.BlockSpec((8, 512), lambda i, p: (0, i)),
                pl.BlockSpec((16, 512), lambda i, p: (0, i)),
            ],
            out_specs=[
                pl.BlockSpec((1, 4, 144, 512), lambda i, p: (i ^ p[0], 0, 0, 0)),
                pl.BlockSpec((4, 1, 128, 512), lambda i, p: (0, i ^ p[0], 0, 0)),
            ],
        ),
        out_shape=[
            jax.ShapeDtypeStruct((4, 4, 144, 512), BF16),
            jax.ShapeDtypeStruct((4, 4, 128, 512), BF16),
        ],
        compiler_params=PARAMS,
        cost_estimate=cost(40e9, 16),
    )(place, n, *dh, df, o, first_all, total, small, sums)


def scores_of(info_ref, slopes_ref, seq, head, query, keys):
    n = query.shape[0]
    flip_half = info_ref[8]
    row = lax.broadcasted_iota(jnp.int32, (n, 1), 0)
    col = lax.broadcasted_iota(jnp.int32, (1, n), 1)
    row = row ^ (flip_half * 128)
    col = col ^ (flip_half * 128)
    raw = lax.dot_general(query, keys, (((1,), (1,)), ((), ())), preferred_element_type=F32)
    distance = jnp.abs(row - col).astype(F32)
    s = raw * SCALE - slopes_ref[head] * distance
    allowed = col <= row
    place = (info_ref[9] ^ (seq % 2)) * 2 + (info_ref[10] ^ (seq // 2))
    for p in range(2):
        start = info_ref[place * 2 + p]
        in_row = (row >= start) & (row < start + PIECE)
        in_col = (col >= start) & (col < start + PIECE)
        allowed = allowed | (in_row & in_col)
    return jnp.where(allowed, s, -1e30)


def store_partial(out_refs, values):
    own_ref, near_ref, beyond_ref = out_refs
    step = pl.program_id(0)
    values = values.astype(BF16)

    @pl.when(step < 2)
    def _():
        own_ref[...] = values

    @pl.when(step == 2)
    def _():
        near_ref[...] = values

    @pl.when(step == 3)
    def _():
        beyond_ref[...] = values


PARTIAL_SPECS = [
    pl.BlockSpec((256, 2048), lambda i: (jnp.minimum(i, 1), 0)),
    pl.BlockSpec((256, 2048), lambda i: (0, 0)),
    pl.BlockSpec((256, 2048), lambda i: (0, 0)),
]
PARTIAL = [like(512, BF16), like(256, BF16), like(256, BF16)]


def forward_kernel(
    info_ref, slopes_ref, v0_ref, v1_ref, small_ref, bias_ref, w_ref, n_ref, f_ref, o_ref, *out_refs
):
    seq = pl.program_id(0)
    n = (pick(v0_ref, v1_ref) * small_ref[0:1] + small_ref[1:2]).astype(BF16)
    n_ref[...] = n
    weight = w_ref[...].reshape(2048, 1024)
    f = (jnp.dot(n, weight[:, :768], preferred_element_type=F32) + bias_ref[...]).astype(BF16)
    f_ref[...] = f
    mixed = []
    for head in range(2):
        q, k, v = (f[:, (head * 3 + i) * HD : (head * 3 + i + 1) * HD] for i in range(3))
        s = scores_of(info_ref, slopes_ref, seq, head, q, k)
        top = jnp.max(s, axis=-1, keepdims=True)
        e = jnp.exp(s - top)
        prob = (e / jnp.sum(e, axis=-1, keepdims=True)).astype(BF16)
        mixed.append(jnp.dot(prob, v, preferred_element_type=F32).astype(BF16))
    mixed = jnp.concatenate(mixed, axis=1)
    o_ref[...] = mixed
    store_partial(out_refs, contract_cols(mixed, weight[:, 768:]))


def backward_kernel(info_ref, slopes_ref, f_ref, own_ref, other_ref, w_ref, df_ref, sum_ref):
    seq = pl.program_id(0)

    @pl.when(seq == 0)
    def _():
        sum_ref[...] = jnp.zeros_like(sum_ref)

    dh = pick(own_ref, other_ref)
    grad = jnp.dot(dh, w_ref[...].reshape(2048, 256), preferred_element_type=F32).astype(BF16)
    for head in range(2):
        base = head * 3 * HD
        q = f_ref[:, base : base + HD]
        k = f_ref[:, base + HD : base + 2 * HD]
        v = f_ref[:, base + 2 * HD : base + 3 * HD]
        g = grad[:, head * HD : (head + 1) * HD]
        s = scores_of(info_ref, slopes_ref, seq, head, q, k)
        top = jnp.max(s, axis=-1, keepdims=True)
        e = jnp.exp(s - top)
        prob = e / jnp.sum(e, axis=-1, keepdims=True)
        dp = contract_cols(g, v)
        row_dot = jnp.sum(prob * dp, axis=-1, keepdims=True)
        ds = (prob * (dp - row_dot) * SCALE).astype(BF16)
        dq = jnp.dot(ds, k, preferred_element_type=F32)
        dk = contract_rows(ds, q)
        dv = contract_rows(prob.astype(BF16), g)
        for i, part in enumerate((dq, dk, dv)):
            at = base + i * HD
            df_ref[:, at : at + HD] = part.astype(BF16)
            sum_ref[0:1, at : at + HD] += jnp.sum(part, axis=0, keepdims=True)


def norm_one_kernel(df_ref, w_ref, *out_refs):
    store_partial(out_refs, contract_cols(df_ref[...], w_ref[...].reshape(2048, 768)))


def forward_attention(info, slopes, vhat, small, bias, first_all):
    rows = 1024
    return pl.pallas_call(
        forward_kernel,
        grid=(rows // 256,),
        in_specs=[
            SCALARS, SCALARS, *halves(256, 2048), whole(8, 2048), whole(1, 768), whole(16, 128, 1024),
        ],
        out_specs=[row_block(2048), row_block(768), row_block(256), *PARTIAL_SPECS],
        out_shape=[
            like(rows, BF16),
            jax.ShapeDtypeStruct((rows, 768), BF16),
            jax.ShapeDtypeStruct((rows, 256), BF16),
            *PARTIAL,
        ],
        compiler_params=PARAMS,
        cost_estimate=cost(10e9, 24),
    )(info, slopes, *vhat, small, bias, first_all)


def backward_attention(info, slopes, f, dh, first_all):
    rows = f.shape[0]
    return pl.pallas_call(
        backward_kernel,
        grid=(rows // 256,),
        in_specs=[
            SCALARS,
            SCALARS,
            row_block(768),
            *halves(256, 2048),
            pl.BlockSpec((16, 128, 256), lambda i: (0, 0, 3)),
        ],
        out_specs=[row_block(768), whole(8, 768)],
        out_shape=[
            jax.ShapeDtypeStruct((rows, 768), BF16),
            jax.ShapeDtypeStruct((8, 768), F32),
        ],
        compiler_params=PARAMS,
        cost_estimate=cost(64e9, 10),
    )(info, slopes, f, *dh, first_all)


def norm_one_partial_of(df, first_all):
    rows = df.shape[0]
    return pl.pallas_call(
        norm_one_kernel,
        grid=(rows // 256,),
        in_specs=[row_block(768), whole(16, 128, 768)],
        out_specs=PARTIAL_SPECS,
        out_shape=PARTIAL,
        compiler_params=PARAMS,
        cost_estimate=cost(16e9, 10),
    )(df, first_all)


def unit_kernel(n0_ref, n1_ref, c0_ref, c1_ref, w_ref, bias_ref, a_ref, du_ref, sum_ref, *out_refs):
    @pl.when(pl.program_id(0) == 0)
    def _():
        sum_ref[...] = jnp.zeros_like(sum_ref)

    n, cot = pick(n0_ref, n1_ref), pick(c0_ref, c1_ref).reshape(256, 2048)
    total = None
    for j in range(2):
        cols = slice(j * 512, j * 512 + 512)
        w_up, w_down = w_ref[:, cols], w_ref[:, 1024 + j * 512 : 1536 + j * 512]
        u = jnp.dot(n, w_up, preferred_element_type=F32) + bias_ref[:, cols]
        da = jnp.dot(cot, w_down, preferred_element_type=F32)
        a_ref[:, cols] = gelu_tanh(u).astype(BF16)
        du = da * gelu_slope(u)
        sum_ref[0:1, cols] += jnp.sum(du, axis=0, keepdims=True)
        du = du.astype(BF16)
        du_ref[:, cols] = du
        part = contract_cols(du, w_up)
        total = part if total is None else total + part
    store_partial(out_refs, total)


def units(n, packed, second_all, bias):
    rows = 1024
    return pl.pallas_call(
        unit_kernel,
        grid=(rows // 256,),
        in_specs=[
            *halves(256, 2048),
            pl.BlockSpec((2, 1, 128, 2048), lambda i: (jnp.minimum(i, 1), 1, 0, 0)),
            pl.BlockSpec((2, 1, 128, 2048), lambda i: (jnp.maximum(i - 2, 0), 1, 0, 0)),
            whole(2048, 2048),
            whole(1, 1024),
        ],
        out_specs=[row_block(1024), row_block(1024), whole(8, 1024), *PARTIAL_SPECS],
        out_shape=[
            jax.ShapeDtypeStruct((rows, 1024), BF16),
            jax.ShapeDtypeStruct((rows, 1024), BF16),
            jax.ShapeDtypeStruct((8, 1024), F32),
            *PARTIAL,
        ],
        compiler_params=PARAMS,
        cost_estimate=cost(18e9, 24),
    )(*n, *packed, second_all, bias)


def unit_output_kernel(a_ref, w_ref, *out_refs):
    store_partial(out_refs, contract_cols(a_ref[...], w_ref[...]))


def unit_output(a, second_all):
    rows = a.shape[0]
    return pl.pallas_call(
        unit_output_kernel,
        grid=(rows // 256,),
        in_specs=[row_block(1024), pl.BlockSpec((2048, 1024), lambda i: (0, 1))],
        out_specs=PARTIAL_SPECS,
        out_shape=PARTIAL,
        compiler_params=PARAMS,
        cost_estimate=cost(6e9, 12),
    )(a, second_all)


def body(
    tokens,
    piece_starts,
    ln1_gain,
    ln1_bias,
    qkv_weight,
    qkv_bias,
    out_weight,
    out_bias,
    ln2_gain,
    ln2_bias,
    up_weight,
    up_bias,
    down_weight,
    down_bias,
    cotangent,
):
    xh, c, t = lax.axis_index("xh"), lax.axis_index("c"), lax.axis_index("t")
    quarter = xh * 2 + c

    me = quarter.reshape(1).astype(jnp.int32)
    small_own = small_block(
        (ln1_gain, ln1_bias, out_bias, ln2_gain, ln2_bias, down_bias), qkv_bias, up_bias, piece_starts, xh, c, t
    )
    first_rows = spread_columns(me, [qkv_weight, out_weight], extra=small_own)
    first_all = lax.all_gather(first_rows, PLANE, axis=0)
    packed = whole_call(pack_kernel, like(256, BF16), tokens, cotangent)
    came = gather_start(packed)
    onward = gather_split(came)
    second_rows = spread_columns(me, [up_weight, down_weight], onward[0])
    second_all = lax.all_gather(second_rows, PLANE, axis=0, tiled=True)

    starts = first_rows[138, :8].astype(jnp.int32)
    info = jnp.concatenate([starts, jnp.stack([t, xh, c]).astype(jnp.int32)])
    head_ids = t * 8 + quarter * 2 + jnp.arange(2, dtype=jnp.int32)
    slopes = jnp.exp2(-8.0 * (head_ids.astype(F32) + 1.0) / H)

    own, other = gather_finish(packed, came, gather_onward(onward), second_rows)
    packed = own.reshape(4, 2, 128, 2048), other.reshape(4, 2, 128, 2048)
    vhat = [first_norm(v) for v in packed]
    small, bias_joined, bias_up = small_vectors(first_all[:, 128:], quarter, t)
    normed_all, f, mixed, own, *far = forward_attention(
        info, slopes, vhat, small, bias_joined, first_all
    )
    beyond, near = swap_cores(far)
    sums = [(own, near, beyond)]
    from1, from3 = ring_next(sums, ring_two(sums))
    middle, normed_two = small_call(
        middle_kernel,
        [((128, 2048), F32), ((128, 2048), BF16)],
        [own[:128], near[:128], from1, from3, tokens, small],
    )
    normed_two_all = gather_group(normed_two)
    active, hidden_grad, unit_sums, own, *far = units(normed_two_all, packed, second_all, bias_up)

    beyond, near = swap_cores(far)
    sums = [(own, near, beyond)]
    from1, from3 = ring_next(sums, ring_two(sums))
    second_out, done = up_grads(normed_two_all, hidden_grad)
    middle_grad, branch_grad, row_sums = small_call(
        second_back_kernel,
        [((128, 2048), F32), ((128, 2048), BF16), ((8, 2048), F32)],
        [own[:128], near[:128], from1, from3, middle, cotangent, small],
        done,
    )
    came = gather_start(branch_grad)
    second_out, done = down_grads(second_out, packed, active)
    second_grads = lax.psum_scatter(second_out, PLANE, scatter_dimension=0, tiled=True)
    onward = gather_split(came, done)
    out_own, *out_far = unit_output(active, second_all)
    branch_grad_all = gather_finish(branch_grad, came, gather_onward(onward), out_far[1])
    out_beyond, out_near = swap_cores(out_far)

    joined_grad, joined_sums = backward_attention(
        info, slopes, f, branch_grad_all, first_all
    )
    place = jnp.stack([lax.axis_index("z"), lax.axis_index("y")]).astype(jnp.int32)
    sums = jnp.concatenate(
        [
            row_sums[:6],
            bias_rows(joined_sums[0:1], quarter, t),
            bias_rows(unit_sums[0:1], quarter, t),
            jnp.zeros((3, 2048), F32),
        ],
        axis=0,
    )
    grads_z, grads_y = first_grads_of(
        place, normed_all, branch_grad_all, joined_grad, mixed, first_all, joined_sums, small, sums
    )

    blocks = grads_z.reshape(4, 576, 512), grads_y.reshape(4, 512, 512)
    came = (
        axis_swap(blocks[0][2, :288], "z", 1),
        axis_swap(blocks[0][2, 288:], "z", 3),
        axis_swap(blocks[1][2, :256], "y", 1),
        axis_swap(blocks[1][2, 256:], "y", 3),
    )
    one_own, *one_far = norm_one_partial_of(joined_grad, first_all)
    one_beyond, one_near = swap_cores(one_far)
    came = axis_next(("z", "y"), blocks, came, one_far[1])
    both = [(one_own, one_near, one_beyond), (out_own, out_near, out_beyond)]
    add3, add1 = ring_two(both)
    from1, from3 = ring_next(both, (add3, add1))
    blocks, came = axis_turn(blocks[0][0], blocks[1][0], came, add3)
    came = axis_next(("y", "z"), blocks, came)
    sent = small_call(
        return_kernel,
        [((48, 3072), BF16)] * 4,
        [blocks[0], *came[:2], blocks[1], *came[2:], second_grads],
        from1,
        from3,
        scalars=me,
    )
    terms = (
        [one_own[:128], one_near[:128], from1[:128], from3[:128]],
        [out_own[:128], out_near[:128], from1[128:], from3[128:]],
    )
    (grad_tokens,) = small_call(
        first_back_kernel, [((128, 2048), F32)], [*terms[0], tokens, middle_grad, small]
    )
    (layer_out,) = small_call(output_kernel, [((128, 2048), BF16)], [*terms[1], middle, small])

    grad_qkv, grad_out, grad_up, grad_down, mine = small_call(
        place_kernel,
        [((32, 3072), F32), ((32, 1024), F32), ((32, 4096), F32), ((32, 4096), F32), ((16, 128), F32)],
        exchange(*sent),
        scalars=me,
    )
    mine = mine + swap_x(mine, 1)
    mine = lax.dynamic_slice_in_dim(mine, quarter * 32 + t * 16, 16, 1)

    return (
        layer_out,
        grad_tokens,
        mine[4],
        mine[5],
        grad_qkv,
        mine[6:9].reshape(48),
        grad_out,
        mine[0],
        mine[1],
        mine[2],
        grad_up,
        mine[9:13].reshape(64),
        grad_down,
        mine[3],
    )


def solution(mesh):
    fine = Mesh(mesh.devices.reshape(2, 4, 4, 2, 2), AXES)
    dp = ("xh", "z", "y", "c")
    rows, vec, mat = P(AXES, None), P(AXES), P(dp, "t")
    return jax.shard_map(
        body,
        mesh=fine,
        in_specs=(
            rows, P(dp, None), vec, vec, mat, vec, mat, vec, vec, vec, mat, vec, mat, vec, rows,
        ),
        out_specs=(
            rows, rows, vec, vec, mat, vec, mat, vec, vec, vec, mat, vec, mat, vec,
        ),
        check_vma=False,
    )
```

```python
import functools
import functools
import math

import jax
import jax.numpy as jnp
from jax import lax
from jax.experimental import pallas as pl
from jax.experimental.pallas import tpu as pltpu
from jax.sharding import Mesh
from jax.sharding import PartitionSpec as P

H = 16
HD = 128
PIECE = 64
EPS = 1e-05
GELU_COEF = math.sqrt(2.0 / math.pi)
SCALE = 1.0 / math.sqrt(HD)

AXES = ("xh", "z", "y", "c", "t")
RING = ("xh", "t")
PLANE = ("z", "y")
BF16 = jnp.bfloat16
F32 = jnp.float32


def gelu_tanh(values):
    return (
        0.5 * values * (1.0 + jnp.tanh(GELU_COEF * (values + 0.044715 * values * values * values)))
    )


def gelu_slope(values):
    square = values * values
    inner = jnp.tanh(GELU_COEF * (values + 0.044715 * values * square))
    return 0.5 * (1.0 + inner) + 0.5 * values * (1.0 - inner * inner) * GELU_COEF * (
        1.0 + 3.0 * 0.044715 * square
    )


def contract_rows(left_side, right_side):
    return lax.dot_general(
        left_side, right_side, (((0,), (0,)), ((), ())), preferred_element_type=F32
    )


def contract_cols(left_side, right_side):
    return lax.dot_general(
        left_side, right_side, (((1,), (1,)), ((), ())), preferred_element_type=F32
    )


def swap_x(v, mask):
    return lax.ppermute(v, RING, [(i, i ^ mask) for i in range(4)])


def swap_c(v):
    return lax.ppermute(v, "c", [(0, 1), (1, 0)])


ANYWHERE = pl.BlockSpec(memory_space=pl.ANY)
ENTIRE = pl.BlockSpec()
SCALARS = pl.BlockSpec(memory_space=pltpu.SMEM)


def far(*arrays):
    return [pltpu.with_memory_space_constraint(v, pltpu.HBM) for v in arrays]


def part(array, block, *index):
    return pltpu.with_memory_space_constraint(array, pltpu.HBM), pl.BlockSpec(block, lambda _: index)


def small_call(kernel, outs, operands, *others, scalars=None, token=False):
    first = [] if scalars is None else [scalars]
    outs = [*outs, ((8, 128), F32)] if token else outs
    operands = [v if isinstance(v, tuple) else (v, ENTIRE) for v in operands]

    def run(*refs):
        used = len(first) + len(operands)
        if token:
            *refs, done_ref = refs
            done_ref[...] = jnp.zeros_like(done_ref)
        kernel(*refs[:used], *refs[used + len(others) :])

    return pl.pallas_call(
        run,
        grid=(1,),
        in_specs=[SCALARS] * len(first) + [spec for _, spec in operands] + [ANYWHERE] * len(others),
        out_specs=[ENTIRE] * len(outs),
        out_shape=[
            (pltpu.HBM if math.prod(shape) * (2 if dtype == F32 else 1) > 2**18 else jax.ShapeDtypeStruct)(
                shape, dtype
            )
            for shape, dtype in outs
        ],
        compiler_params=pltpu.CompilerParams(vmem_limit_bytes=24 << 20),
        cost_estimate=pl.CostEstimate(flops=0, bytes_accessed=4 << 20, transcendentals=0),
    )(*first, *(v for v, _ in operands), *others)


def block_of(array, index):
    return array, pl.BlockSpec((128, 2048), lambda _: (index, 0))


def gate_kernel(*refs):
    pass


def joined(values, *others):
    return pl.pallas_call(
        gate_kernel,
        in_specs=[ANYWHERE] * (len(values) + len(others)),
        out_specs=[ANYWHERE] * len(values),
        out_shape=[pltpu.HBM(v.shape, v.dtype) for v in values],
        input_output_aliases={i: i for i in range(len(values))},
        cost_estimate=pl.CostEstimate(flops=0, bytes_accessed=0, transcendentals=0),
    )(*values, *others)


def split_kernel(one_ref, three_ref, low_ref, high_ref):
    half = low_ref.shape[0]
    low_ref[...] = three_ref[:half]
    high_ref[...] = one_ref[half:]


def pile_kernel(*refs):
    *pieces, out_ref = refs
    at = 0
    for piece in pieces:
        rows = piece.shape[0]
        out_ref[at : at + rows] = piece[...]
        at += rows


def gather_start(v):
    return swap_x(v, 1), swap_x(v, 3)


def gather_split(came, *others):
    rows, width = came[0].shape
    return small_call(split_kernel, [((rows // 2, width), BF16)] * 2, came, *others)


def gather_onward(onward):
    return swap_x(onward[0], 1), swap_x(onward[1], 3)


def gather_finish(v, came, opposite, *others):
    rows, width = v.shape
    pieces = [v, came[0], *opposite, came[1]]
    (own,) = small_call(pile_kernel, [((4 * rows, width), BF16)], pieces, *others)
    return own, swap_c(own)


def gather_group(v):
    came = gather_start(v)
    return gather_finish(v, came, gather_onward(gather_split(came)))


def add_low(*values):
    return sum(v.astype(F32) for v in values).astype(BF16)


def swap_cores(far):
    near, beyond = far
    return swap_c(beyond), swap_c(near)


def ring_two_kernel(own, beyond, low_ref, high_ref):
    two = add_low(own[...], beyond[...])
    half = low_ref.shape[0]
    low_ref[...] = two[:half]
    high_ref[...] = two[half:]


def ring_two(sums, *others):
    own, _, beyond = sums
    outs = [((64, 2048), BF16)] * 2
    ins = [part(own, (128, 2048), 2, 0), block_of(beyond, 0)]
    low, high = small_call(ring_two_kernel, outs, ins, *others)
    return swap_x(low, 1), swap_x(high, 3)


def ring_next_kernel(own1, own3, near, beyond, add3_ref, add1_ref, s1_ref, s3_ref):
    half = add3_ref.shape[0]
    s3_ref[:half] = add_low(own3[:half], beyond[:half], add3_ref[...])
    s3_ref[half:] = add_low(own3[half:], beyond[half:])
    s1_ref[:half] = add_low(own1[:half], near[:half])
    s1_ref[half:] = add_low(own1[half:], near[half:], add1_ref[...])


def ring_next(sums, came, *others):
    own, near, beyond = sums
    own1, own3 = part(own, (128, 2048), 1, 0), part(own, (128, 2048), 3, 0)
    ins = [own1, own3, block_of(near, 1), block_of(beyond, 1), *came]
    return small_call(ring_next_kernel, [((128, 2048), BF16)] * 2, ins, *others)


def ring_last(sent):
    return swap_x(sent[0], 1), swap_x(sent[1], 3)


def axis_swap(v, axis, mask):
    return lax.ppermute(v, axis, [(i, i ^ mask) for i in range(4)])


def axis_next_kernel(a1, a3, add3_a, add1_a, b1, b3, add3_b, add1_b, *outs):
    for (one, three, add3, add1), (one_ref, three_ref) in (
        ((a1, a3, add3_a, add1_a), outs[:2]),
        ((b1, b3, add3_b, add1_b), outs[2:]),
    ):
        half = add3.shape[0]
        three_ref[:half] = add_low(three[0, :half], add3[...])
        three_ref[half:] = three[0, half:]
        one_ref[:half] = one[0, :half]
        one_ref[half:] = add_low(one[0, half:], add1[...])


def axis_next(axes, blocks, came, *others):
    a, b = blocks
    outs = [((a.shape[1], 512), BF16)] * 2 + [((b.shape[1], 512), BF16)] * 2
    pick = lambda v, i: part(v, (1, *v.shape[1:]), i, 0, 0)
    ins = [pick(a, 1), pick(a, 3), *came[:2], pick(b, 1), pick(b, 3), *came[2:]]
    one_a, three_a, one_b, three_b = small_call(axis_next_kernel, outs, ins, *others)
    return (
        axis_swap(one_a, axes[0], 1),
        axis_swap(three_a, axes[0], 3),
        axis_swap(one_b, axes[1], 1),
        axis_swap(three_b, axes[1], 3),
    )


def axis_turn_kernel(a_ref, a1, a3, b_ref, b1, b3, *outs):
    sum_a = add_low(a_ref[0], a1[...], a3[...]).reshape(4, 144, 512)
    sum_b = add_low(b_ref[0], b1[...], b3[...]).reshape(4, 128, 512)
    for i in range(4):
        outs[i][...] = sum_a[i]
        outs[4 + i][...] = sum_b[i]


def axis_turn(a, b, came, *others):
    ins = [part(a, (1, 576, 512), 0, 0, 0), *came[:2], part(b, (1, 512, 512), 0, 0, 0), *came[2:]]
    outs = [((144, 512), BF16)] * 4 + [((128, 512), BF16)] * 4
    own = small_call(axis_turn_kernel, outs, ins, *others)
    sum_a, sum_b = own[:4], own[4:]
    terms_a = [sum_a[0], *(axis_swap(sum_a[i], "y", i) for i in (2, 1, 3))]
    terms_b = [sum_b[0], *(axis_swap(sum_b[i], "z", i) for i in (2, 1, 3))]
    return terms_a, terms_b


def exchange(own, near, far, cross):
    return (
        own,
        swap_c(near),
        lax.ppermute(far, "xh", [(0, 1), (1, 0)]),
        lax.ppermute(cross, ("xh", "c"), [(i, 3 - i) for i in range(4)]),
    )


def spread_kernel(me_ref, *refs):
    parts, outs = refs[:-4], refs[-4:]
    for other, out_ref in enumerate(outs):
        quarter = me_ref[0] ^ other
        at = 0
        for part_ref in parts:
            if part_ref.shape[0] == 32:
                width = part_ref.shape[1] // 4
                start = pl.multiple_of(quarter * width, 128)
                out_ref[:32, at : at + width] = part_ref[:, pl.ds(start, width)]
                at += width
            else:
                out_ref[32:] = part_ref[...]


def collect_kernel(me_ref, *refs):
    *came, out_ref = refs
    for other, part_ref in enumerate(came):
        start = pl.multiple_of((me_ref[0] ^ other) * 32, 32)
        out_ref[pl.ds(start, 32)] = part_ref[:32]
    if out_ref.shape[0] > 128:
        out_ref[128:] = add_low(*(part_ref[32:] for part_ref in came))


def spread_columns(me, parts, *others, extra=None):
    below = 0 if extra is None else 16
    width = sum(p.shape[1] for p in parts) // 4
    ins = far(*parts) if extra is None else [*far(*parts), extra]
    sent = small_call(spread_kernel, [((32 + below, width), BF16)] * 4, ins, *others, scalars=me)
    (rows,) = small_call(
        collect_kernel, [((128 + below, width), BF16)], exchange(*sent), scalars=me
    )
    return rows


def rows_kernel(me_ref, rows_ref, *outs):
    for other, out_ref in enumerate(outs):
        start = pl.multiple_of((me_ref[0] ^ other) * 32, 32)
        out_ref[...] = rows_ref[pl.ds(start, 32)]


def return_kernel(me_ref, *refs):
    terms, outs = refs[:8], refs[8:]
    sum_a = add_low(*(v[...] for v in terms[:4]))
    sum_b = add_low(*(v[...] for v in terms[4:]))
    for at in range(4):
        rows = slice(at * 32, at * 32 + 32)

        for other, out_ref in enumerate(outs):

            @pl.when(me_ref[0] ^ other == at)
            def _():
                out_ref[:32, :512] = sum_a[rows]
                out_ref[:32, 512:] = sum_b[rows]

    for out_ref in outs:
        out_ref[32:, :512] = sum_a[128:]
        out_ref[32:, 512:] = jnp.zeros((16, 512), BF16)


def place_kernel(widths, me_ref, *refs):
    came, outs = refs[:4], refs[4:]
    for other, part_ref in enumerate(came):
        quarter = me_ref[0] ^ other
        at = 0
        for ref, width in zip(outs, widths):
            start = pl.multiple_of(quarter * width, 128)
            ref[:, pl.ds(start, width)] = part_ref[:32, at : at + width].astype(F32)
            at += width
    if len(outs) > len(widths):
        outs[-1][...] = sum(part_ref[32:, :256].astype(F32) for part_ref in came)


def two_pieces(v):
    high = lax.reduce_precision(v, 8, 7)
    return jnp.stack([high, v - high]).astype(BF16)


def small_block(vectors, joined_bias, unit_bias, starts, xh, c, t):
    flat = jnp.concatenate([*vectors, joined_bias, unit_bias])
    other = swap_x(flat, 1)
    pair = jnp.where(t == 0, jnp.stack([flat, other]), jnp.stack([other, flat]))
    pieces = two_pieces(pair)
    mine = (jnp.arange(4) == xh * 2 + c).astype(BF16)
    rows = pieces[:, :, :96].reshape(2, 2, 6, 16).transpose(2, 0, 1, 3).reshape(6, 2, 1, 32)
    rows = (rows * mine[:, None]).reshape(6, 256)
    joined = (pieces[:, :, 96:144].reshape(2, 1, 96) * mine[:, None]).reshape(2, 384)
    unit = (pieces[:, :, 144:].reshape(2, 1, 128) * mine[:, None]).reshape(2, 512)
    starts = (starts.astype(BF16) * mine[:, None]).reshape(1, 8)
    wide = lambda v: jnp.pad(v, ((0, 0), (0, 1024 - v.shape[1])))
    return jnp.concatenate(
        [wide(rows), wide(joined), wide(unit), wide(starts), jnp.zeros((5, 1024), BF16)], axis=0
    )


def small_vectors(gathered, quarter, t):
    rows = gathered[:, :8, :256].astype(F32)
    rows = (rows[:, :, :128] + rows[:, :, 128:]).transpose(1, 0, 2).reshape(8, 2048)
    take = lambda first, width: (
        lax.dynamic_slice(gathered, (quarter * 4, first, t * width), (4, 2, width))
        .astype(F32)
        .sum(axis=1)
        .reshape(1, 4 * width)
    )
    return rows, take(6, 192), take(8, 256)


def low_half(rows):
    return lax.broadcasted_iota(jnp.int32, (rows, 128), 1) < 64


def store_plane(ref, values):
    low = low_half(values.shape[0])
    for j in range(8):
        a = values[:, j * 128 : j * 128 + 128]
        b = values[:, 1024 + j * 128 : 1024 + j * 128 + 128]
        at = j * 256
        ref[:, at : at + 128] = jnp.where(low, a, pltpu.roll(b, 64, 1)).astype(ref.dtype)
        ref[:, at + 128 : at + 256] = jnp.where(low, pltpu.roll(a, 64, 1), b).astype(ref.dtype)


def natural(values):
    low = low_half(values.shape[0])
    first, second = [], []
    for j in range(8):
        a = values[:, j * 256 : j * 256 + 128]
        b = values[:, j * 256 + 128 : j * 256 + 256]
        first.append(jnp.where(low, a, pltpu.roll(b, 64, 1)))
        second.append(jnp.where(low, pltpu.roll(a, 64, 1), b))
    return jnp.concatenate(first + second, axis=1)


def total_of(refs):
    return natural(sum(r[...].astype(F32) for r in refs))


def row_stats(values):
    centre = values - jnp.mean(values, axis=-1, keepdims=True)
    spread = jnp.mean(centre * centre, axis=-1, keepdims=True)
    return centre, lax.rsqrt(spread + EPS)


def norm_back(values, gain, upstream):
    centre, scale = row_stats(values)
    vhat = centre * scale
    e = upstream * gain
    dv = scale * (
        e - jnp.mean(e, axis=-1, keepdims=True) - vhat * jnp.mean(e * vhat, axis=-1, keepdims=True)
    )
    return dv, vhat


def first_norm_kernel(x_ref, n_ref, done_ref):
    done_ref[...] = jnp.zeros_like(done_ref)
    centre, scale = row_stats(x_ref[...].astype(F32))
    store_plane(n_ref, centre * scale)


def middle_kernel(t0, t1, t2, t3, x_ref, small_ref, mid_ref, n_ref):
    small = natural(small_ref[...])
    middle = x_ref[...].astype(F32) + (total_of((t0, t1, t2, t3)) + small[2:3])
    mid_ref[...] = middle
    centre, scale = row_stats(middle)
    store_plane(n_ref, centre * scale * small[3:4] + small[4:5])


def second_back_kernel(t0, t1, t2, t3, mid_ref, cot_ref, small_ref, dh_ref, low_ref, sum_ref):
    small = natural(small_ref[...])
    upstream = total_of((t0, t1, t2, t3))
    dv, vhat = norm_back(mid_ref[...], small[3:4], upstream)
    final = cot_ref[...].astype(F32)
    dh = final + dv
    dh_ref[...] = dh
    store_plane(low_ref, dh)
    total = lambda v: jnp.sum(v, axis=0, keepdims=True)
    store_plane(
        sum_ref,
        jnp.concatenate(
            [total(dh), total(upstream * vhat), total(upstream), total(final), jnp.zeros((4, 2048), F32)],
            axis=0,
        ),
    )


def first_back_kernel(t0, t1, t2, t3, x_ref, dh_ref, small_ref, g_ref):
    small = natural(small_ref[...])
    dv, _ = norm_back(x_ref[...].astype(F32), small[0:1], total_of((t0, t1, t2, t3)))
    g_ref[...] = dh_ref[...] + dv


def output_kernel(t0, t1, t2, t3, mid_ref, small_ref, o_ref):
    small = natural(small_ref[...])
    o_ref[...] = (mid_ref[...] + (total_of((t0, t1, t2, t3)) + small[5:6])).astype(BF16)


def plane_kernel(x_ref, o_ref):
    store_plane(o_ref, x_ref[...].astype(F32))


PARAMS = pltpu.CompilerParams(vmem_limit_bytes=48 << 20)


def cost(flops, mebibytes):
    return pl.CostEstimate(flops=int(flops), bytes_accessed=int(mebibytes * 2**20), transcendentals=0)


def whole_call(kernel, outs, *operands):
    return pl.pallas_call(
        kernel, out_shape=outs, compiler_params=PARAMS, cost_estimate=cost(0, 4)
    )(*operands)


def row_block(width):
    return pl.BlockSpec((256, width), lambda i: (i, 0))


def whole(*shape):
    return pl.BlockSpec(shape, lambda i: (0,) * len(shape))


def halves(*block):
    tail = (0,) * (len(block) - 1)
    return [
        pl.BlockSpec(block, lambda i: (jnp.minimum(i, 1), *tail)),
        pl.BlockSpec(block, lambda i: (jnp.maximum(i - 2, 0), *tail)),
    ]


def pick(own_ref, other_ref):
    return jnp.where(pl.program_id(0) < 2, own_ref[...], other_ref[...])


def contract_both(own, other, right):
    half = right.shape[0] // 2
    return contract_rows(own, right[:half]) + contract_rows(other, right[half:])


def like(rows, dtype):
    return jax.ShapeDtypeStruct((rows, 2048), dtype)


def first_norm(x):
    return pl.pallas_call(
        first_norm_kernel,
        grid=(2,),
        in_specs=[pl.BlockSpec((256, 2048), lambda i: (i, 0))],
        out_specs=[row_block(2048), whole(8, 128)],
        out_shape=[pltpu.HBM((512, 2048), F32), jax.ShapeDtypeStruct((8, 128), F32)],
        compiler_params=PARAMS,
        cost_estimate=cost(0, 8),
    )(*far(x))


def up_grads_kernel(own_ref, other_ref, du_ref, out_ref, done_ref):
    done_ref[...] = jnp.zeros_like(done_ref)
    out_ref[...] = contract_both(own_ref[...], other_ref[...], du_ref[...]).astype(BF16)


def down_grads_kernel(_, own_ref, other_ref, a_ref, out_ref, done_ref):
    done_ref[...] = jnp.zeros_like(done_ref)
    out_ref[...] = contract_both(own_ref[...], other_ref[...], a_ref[...]).astype(BF16)


def up_grads(n, du):
    rows, width = du.shape
    return pl.pallas_call(
        up_grads_kernel,
        grid=(4,),
        in_specs=[pl.BlockSpec((512, 512), lambda i: (0, i))] * 2 + [whole(rows, width)],
        out_specs=[pl.BlockSpec((512, width), lambda i: (i, 0)), whole(8, 128)],
        out_shape=[
            pltpu.HBM((2048, 2 * width), BF16),
            jax.ShapeDtypeStruct((8, 128), F32),
        ],
        compiler_params=PARAMS,
        cost_estimate=cost(5e9, 10),
    )(*far(*n, du))


def down_grads(left, cot, a):
    rows, width = a.shape
    return pl.pallas_call(
        down_grads_kernel,
        grid=(4,),
        in_specs=[ANYWHERE]
        + [pl.BlockSpec((512, 512), lambda i: (0, i))] * 2
        + [whole(rows, width)],
        out_specs=[pl.BlockSpec((512, width), lambda i: (i, 1)), whole(8, 128)],
        out_shape=[
            pltpu.HBM(left.shape, BF16),
            jax.ShapeDtypeStruct((8, 128), F32),
        ],
        input_output_aliases={0: 0},
        compiler_params=PARAMS,
        cost_estimate=cost(5e9, 10),
    )(left, *far(*cot, a))


def first_grads_kernel(
    place_ref, n_ref, own_ref, other_ref, df_ref, o_ref, w_ref, total_ref, unit_ref, small_ref, sums_ref,
    a_ref, b_ref, al_ref, ah_ref, bl_ref, bh_ref, done_ref
):
    done_ref[...] = jnp.zeros_like(done_ref)
    y = place_ref[1]
    joined = contract_rows(n_ref[...], df_ref[...])
    weight = w_ref[...].reshape(512, 768)
    weighted = joined * weight.astype(F32)
    weighted = sum(weighted[:, j * 128 : j * 128 + 128] for j in range(6))
    weighted = lax.dot_general(
        jnp.ones((8, 128), F32),
        weighted,
        (((1,), (1,)), ((), ())),
        preferred_element_type=F32,
        precision=lax.Precision.HIGHEST,
    )
    shift = contract_cols(total_ref[...].astype(BF16), weight)[0:1]
    gain = (weighted[0:1] - small_ref[1:2] * shift) / small_ref[0:1]
    sums = jnp.concatenate([sums_ref[:4], gain, shift, jnp.zeros((2, 512), F32)], axis=0)
    z = pl.program_id(0)
    z_to = z ^ place_ref[0]
    here = (z == place_ref[2]).astype(F32)
    row = lax.broadcasted_iota(jnp.int32, (8, 256), 0)
    row_of = lambda v, at: jnp.where(row == at, v[0:1, :256] * here, 0.0)
    joined_total = total_ref[...]
    joined = joined.astype(BF16)
    out = contract_both(own_ref[...], other_ref[...], o_ref[...]).astype(BF16)
    for i in range(4):
        rows = slice(i * 128, i * 128 + 128)
        mine = pltpu.roll(joined_total, 768 - i * 192, 1) if i else joined_total
        biases = row_of(mine, place_ref[3]) + row_of(
            unit_ref[:, i * 256 : i * 256 + 256], 2 + place_ref[3]
        )
        low = jnp.concatenate([sums[:, rows], jnp.zeros((8, 384), F32)], axis=1)
        high = jnp.concatenate([biases, jnp.zeros((8, 256), F32)], axis=1)
        below = jnp.concatenate([low, high], axis=0).astype(BF16)
        y_to = i ^ y
        a_ref[0, y_to, :128] = joined[rows, :512]
        a_ref[0, y_to, 128:] = below
        b_ref[y_to, 0, :, :256] = joined[rows, 512:]
        b_ref[y_to, 0, :, 256:] = out[rows]

        for half, (low_ref, high_ref) in enumerate(((al_ref, bl_ref), (ah_ref, bh_ref))):

            @pl.when((z_to == 2) & (y_to // 2 == half))
            def _():
                at = pl.multiple_of((y_to % 2) * 144, 16)
                low_ref[pl.ds(at, 128)] = joined[rows, :512]
                low_ref[pl.ds(at + 128, 16)] = below

            @pl.when((y_to == 2) & (z_to // 2 == half))
            def _():
                at = pl.multiple_of((z_to % 2) * 128, 128)
                high_ref[pl.ds(at, 128), :256] = joined[rows, 512:]
                high_ref[pl.ds(at, 128), 256:] = out[rows]


def first_grads_of(place, n, dh, df, o, first_all, total, unit_total, small, sums):
    rows = n.shape[0]
    return pl.pallas_call(
        first_grads_kernel,
        grid_spec=pltpu.PrefetchScalarGridSpec(
            num_scalar_prefetch=1,
            grid=(4,),
            in_specs=[
                pl.BlockSpec((rows, 512), lambda i, p: (0, i)),
                pl.BlockSpec((512, 512), lambda i, p: (0, i)),
                pl.BlockSpec((512, 512), lambda i, p: (0, i)),
                pl.BlockSpec((rows, 768), lambda i, p: (0, 0)),
                pl.BlockSpec((rows, 256), lambda i, p: (0, 0)),
                pl.BlockSpec((4, 128, 768), lambda i, p: (i, 0, 0)),
                pl.BlockSpec((8, 768), lambda i, p: (0, 0)),
                pl.BlockSpec((8, 1024), lambda i, p: (0, 0)),
                pl.BlockSpec((8, 512), lambda i, p: (0, i)),
                pl.BlockSpec((8, 512), lambda i, p: (0, i)),
            ],
            out_specs=[
                pl.BlockSpec((1, 4, 144, 512), lambda i, p: (i ^ p[0], 0, 0, 0)),
                pl.BlockSpec((4, 1, 128, 512), lambda i, p: (0, i ^ p[0], 0, 0)),
                *(pl.BlockSpec((v, 512), lambda i, p: (0, 0)) for v in (288, 288, 256, 256)),
                pl.BlockSpec((8, 128), lambda i, p: (0, 0)),
            ],
        ),
        out_shape=[
            pltpu.HBM((4, 4, 144, 512), BF16),
            pltpu.HBM((4, 4, 128, 512), BF16),
            *(jax.ShapeDtypeStruct((v, 512), BF16) for v in (288, 288, 256, 256)),
            jax.ShapeDtypeStruct((8, 128), F32),
        ],
        compiler_params=PARAMS,
        cost_estimate=cost(40e9, 16),
    )(place, *far(n, *dh, df, o, first_all), total, unit_total, small, sums)


def scores_of(info_ref, slopes_ref, seq, head, query, keys):
    n = query.shape[0]
    flip_half = info_ref[8]
    row = lax.broadcasted_iota(jnp.int32, (n, 1), 0)
    col = lax.broadcasted_iota(jnp.int32, (1, n), 1)
    row = row ^ (flip_half * 128)
    col = col ^ (flip_half * 128)
    raw = lax.dot_general(query, keys, (((1,), (1,)), ((), ())), preferred_element_type=F32)
    distance = jnp.abs(row - col).astype(F32)
    s = raw * SCALE - slopes_ref[head] * distance
    allowed = col <= row
    place = (info_ref[9] ^ (seq % 2)) * 2 + (info_ref[10] ^ (seq // 2))
    for p in range(2):
        start = info_ref[place * 2 + p]
        in_row = (row >= start) & (row < start + PIECE)
        in_col = (col >= start) & (col < start + PIECE)
        allowed = allowed | (in_row & in_col)
    return jnp.where(allowed, s, -1e30)


def store_partial(out_refs, values):
    own_ref, near_ref, beyond_ref = out_refs
    step = pl.program_id(0)
    values = values.astype(BF16)

    @pl.when(step < 2)
    def _():
        own_ref[...] = values

    @pl.when(step == 2)
    def _():
        near_ref[...] = values

    @pl.when(step == 3)
    def _():
        beyond_ref[...] = values


PARTIAL_SPECS = [
    pl.BlockSpec((256, 2048), lambda i: (jnp.minimum(i, 1), 0)),
    pl.BlockSpec((256, 2048), lambda i: (0, 0)),
    pl.BlockSpec((256, 2048), lambda i: (0, 0)),
]
PARTIAL = [pltpu.HBM((rows, 2048), BF16) for rows in (512, 256, 256)]


def forward_kernel(
    info_ref, slopes_ref, v0_ref, v1_ref, small_ref, bias_ref, w_ref, _, n_ref, f_ref, o_ref, done_ref, *out_refs
):
    seq = pl.program_id(0)
    done_ref[...] = jnp.zeros_like(done_ref)
    n = (pick(v0_ref, v1_ref) * small_ref[0:1] + small_ref[1:2]).astype(BF16)
    n_ref[...] = n
    weight = w_ref[...].reshape(2048, 1024)
    f = (jnp.dot(n, weight[:, :768], preferred_element_type=F32) + bias_ref[...]).astype(BF16)
    f_ref[...] = f
    mixed = []
    for head in range(2):
        q, k, v = (f[:, (head * 3 + i) * HD : (head * 3 + i + 1) * HD] for i in range(3))
        s = scores_of(info_ref, slopes_ref, seq, head, q, k)
        top = jnp.max(s, axis=-1, keepdims=True)
        e = jnp.exp(s - top)
        prob = (e / jnp.sum(e, axis=-1, keepdims=True)).astype(BF16)
        mixed.append(jnp.dot(prob, v, preferred_element_type=F32).astype(BF16))
    mixed = jnp.concatenate(mixed, axis=1)
    o_ref[...] = mixed
    store_partial(out_refs, contract_cols(mixed, weight[:, 768:]))


def backward_kernel(
    info_ref, slopes_ref, f_ref, own_ref, other_ref, w_ref, df_ref, sum_ref, *out_refs
):
    seq = pl.program_id(0)

    @pl.when(seq == 0)
    def _():
        sum_ref[...] = jnp.zeros_like(sum_ref)

    dh = pick(own_ref, other_ref)
    weight = w_ref[...].reshape(2048, 1024)
    grad = jnp.dot(dh, weight[:, 768:], preferred_element_type=F32).astype(BF16)
    for head in range(2):
        base = head * 3 * HD
        q = f_ref[:, base : base + HD]
        k = f_ref[:, base + HD : base + 2 * HD]
        v = f_ref[:, base + 2 * HD : base + 3 * HD]
        g = grad[:, head * HD : (head + 1) * HD]
        s = scores_of(info_ref, slopes_ref, seq, head, q, k)
        top = jnp.max(s, axis=-1, keepdims=True)
        e = jnp.exp(s - top)
        prob = e / jnp.sum(e, axis=-1, keepdims=True)
        dp = contract_cols(g, v)
        row_dot = jnp.sum(prob * dp, axis=-1, keepdims=True)
        ds = (prob * (dp - row_dot) * SCALE).astype(BF16)
        dq = jnp.dot(ds, k, preferred_element_type=F32)
        dk = contract_rows(ds, q)
        dv = contract_rows(prob.astype(BF16), g)
        for i, part in enumerate((dq, dk, dv)):
            at = base + i * HD
            df_ref[:, at : at + HD] = part.astype(BF16)
            sum_ref[0:1, at : at + HD] += jnp.sum(part, axis=0, keepdims=True)
    store_partial(out_refs, contract_cols(df_ref[...], weight[:, :768]))


def forward_attention(info, slopes, vhat, small, bias, first_all, other):
    rows = 1024
    return pl.pallas_call(
        forward_kernel,
        grid=(rows // 256,),
        in_specs=[
            SCALARS, SCALARS, *halves(256, 2048), whole(8, 2048), whole(1, 768), whole(16, 128, 1024), ANYWHERE,
        ],
        out_specs=[row_block(2048), row_block(768), row_block(256), whole(8, 128), *PARTIAL_SPECS],
        out_shape=[
            pltpu.HBM((rows, 2048), BF16),
            pltpu.HBM((rows, 768), BF16),
            pltpu.HBM((rows, 256), BF16),
            jax.ShapeDtypeStruct((8, 128), F32),
            *PARTIAL,
        ],
        compiler_params=PARAMS,
        cost_estimate=cost(10e9, 24),
    )(info, slopes, *far(*vhat), small, bias, *far(first_all), other)


def backward_attention(info, slopes, f, dh, first_all):
    rows = f.shape[0]
    return pl.pallas_call(
        backward_kernel,
        grid=(rows // 256,),
        in_specs=[
            SCALARS,
            SCALARS,
            row_block(768),
            *halves(256, 2048),
            whole(16, 128, 1024),
        ],
        out_specs=[row_block(768), whole(8, 768), *PARTIAL_SPECS],
        out_shape=[
            pltpu.HBM((rows, 768), BF16),
            jax.ShapeDtypeStruct((8, 768), F32),
            *PARTIAL,
        ],
        compiler_params=PARAMS,
        cost_estimate=cost(86e9, 10),
    )(info, slopes, *far(f, *dh, first_all))


def unit_kernel(n0_ref, n1_ref, c0_ref, c1_ref, w_ref, bias_ref, a_ref, du_ref, sum_ref, *out_refs):
    @pl.when(pl.program_id(0) == 0)
    def _():
        sum_ref[...] = jnp.zeros_like(sum_ref)

    n, cot = pick(n0_ref, n1_ref), pick(c0_ref, c1_ref)
    total = None
    for j in range(2):
        cols = slice(j * 512, j * 512 + 512)
        w_up, w_down = w_ref[:, cols], w_ref[:, 1024 + j * 512 : 1536 + j * 512]
        u = jnp.dot(n, w_up, preferred_element_type=F32) + bias_ref[:, cols]
        da = jnp.dot(cot, w_down, preferred_element_type=F32)
        a_ref[:, cols] = gelu_tanh(u).astype(BF16)
        du = da * gelu_slope(u)
        sum_ref[0:1, cols] += jnp.sum(du, axis=0, keepdims=True)
        du = du.astype(BF16)
        du_ref[:, cols] = du
        part = contract_cols(du, w_up)
        total = part if total is None else total + part
    store_partial(out_refs, total)


def units(n, cot, second_all, bias):
    rows = 1024
    return pl.pallas_call(
        unit_kernel,
        grid=(rows // 256,),
        in_specs=[
            *halves(256, 2048),
            *halves(256, 2048),
            whole(2048, 2048),
            whole(1, 1024),
        ],
        out_specs=[row_block(1024), row_block(1024), whole(8, 1024), *PARTIAL_SPECS],
        out_shape=[
            pltpu.HBM((rows, 1024), BF16),
            pltpu.HBM((rows, 1024), BF16),
            jax.ShapeDtypeStruct((8, 1024), F32),
            *PARTIAL,
        ],
        compiler_params=PARAMS,
        cost_estimate=cost(18e9, 24),
    )(*far(*n, *cot, second_all), bias)


def unit_output_kernel(a_ref, w_ref, *out_refs):
    *out_refs, done_ref = out_refs
    done_ref[...] = jnp.zeros_like(done_ref)
    store_partial(out_refs, contract_cols(a_ref[...], w_ref[...]))


def unit_output(a, second_all):
    rows = a.shape[0]
    return pl.pallas_call(
        unit_output_kernel,
        grid=(rows // 256,),
        in_specs=[row_block(1024), pl.BlockSpec((2048, 1024), lambda i: (0, 1))],
        out_specs=[*PARTIAL_SPECS, whole(8, 128)],
        out_shape=[*PARTIAL, jax.ShapeDtypeStruct((8, 128), F32)],
        compiler_params=PARAMS,
        cost_estimate=cost(6e9, 12),
    )(*far(a, second_all))


def body(
    tokens,
    piece_starts,
    ln1_gain,
    ln1_bias,
    qkv_weight,
    qkv_bias,
    out_weight,
    out_bias,
    ln2_gain,
    ln2_bias,
    up_weight,
    up_bias,
    down_weight,
    down_bias,
    cotangent,
):
    xh, c, t = lax.axis_index("xh"), lax.axis_index("c"), lax.axis_index("t")
    quarter = xh * 2 + c

    me = quarter.reshape(1).astype(jnp.int32)
    small_own = small_block(
        (ln1_gain, ln1_bias, out_bias, ln2_gain, ln2_bias, down_bias), qkv_bias, up_bias, piece_starts, xh, c, t
    )
    first_rows = spread_columns(me, [qkv_weight, out_weight], extra=small_own)
    first_all = lax.all_gather(first_rows, PLANE, axis=0)
    second_rows = spread_columns(me, [up_weight, down_weight])
    second_all = lax.all_gather(second_rows, PLANE, axis=0, tiled=True)

    starts = first_rows[138, :8].astype(jnp.int32)
    info = jnp.concatenate([starts, jnp.stack([t, xh, c]).astype(jnp.int32)])
    head_ids = t * 8 + quarter * 2 + jnp.arange(2, dtype=jnp.int32)
    slopes = jnp.exp2(-8.0 * (head_ids.astype(F32) + 1.0) / H)

    came = gather_start(tokens)
    onward = gather_split(came, second_rows)
    tokens_all = gather_finish(tokens, came, gather_onward(onward))
    cot_plane = whole_call(plane_kernel, like(128, BF16), cotangent)
    came = gather_start(cot_plane)
    (vhat_own, _), (vhat_other, done) = first_norm(tokens_all[0]), first_norm(tokens_all[1])
    onward = gather_split(came, done)
    opposite = gather_onward(onward)
    vhat = vhat_own, vhat_other
    small, bias_joined, bias_up = small_vectors(first_all[:, 128:], quarter, t)
    normed_all, f, mixed, done, own, *other_core = forward_attention(
        info, slopes, vhat, small, bias_joined, first_all, onward[1]
    )
    cot_all = gather_finish(cot_plane, came, opposite, done)
    beyond, near = swap_cores(joined(other_core, cot_all[0]))
    sums = own, near, beyond
    from1, from3 = ring_last(ring_next(sums, ring_two(sums)))
    middle, normed_two = small_call(
        middle_kernel,
        [((128, 2048), F32), ((128, 2048), BF16)],
        [part(own, (128, 2048), 0, 0), block_of(near, 0), from1, from3, tokens, small],
    )
    normed_two_all = gather_group(normed_two)
    active, hidden_grad, unit_sums, own, *other_core = units(normed_two_all, cot_all, second_all, bias_up)

    beyond, near = swap_cores(other_core)
    sums = own, near, beyond
    came = ring_two(sums)
    second_out, done = up_grads(normed_two_all, hidden_grad)
    from1, from3 = ring_last(ring_next(sums, came, done))
    second_out, done = down_grads(second_out, cot_all, active)
    second_grads = lax.psum_scatter(second_out, PLANE, scatter_dimension=0, tiled=True)
    middle_grad, branch_grad, row_sums = small_call(
        second_back_kernel,
        [((128, 2048), F32), ((128, 2048), BF16), ((8, 2048), F32)],
        [part(own, (128, 2048), 0, 0), block_of(near, 0), from1, from3, middle, cotangent, small],
        done,
    )
    came = gather_start(branch_grad)
    out_own, *out_far, done = unit_output(active, second_all)
    onward = gather_split(came, done)
    branch_grad_all = gather_finish(branch_grad, came, gather_onward(onward))
    out_beyond, out_near = swap_cores(out_far)
    out_sums = out_own, out_near, out_beyond
    out_came = ring_two(out_sums)

    joined_grad, joined_sums, one_own, *one_far = backward_attention(
        info, slopes, f, branch_grad_all, first_all
    )
    out_sent = ring_next(out_sums, out_came, joined_sums)
    out_from1, out_from3 = ring_last(out_sent)
    one_beyond, one_near = swap_cores(joined(one_far, out_sent[1]))
    one_sums = one_own, one_near, one_beyond
    one_came = ring_two(one_sums)
    place = jnp.stack([lax.axis_index("z"), lax.axis_index("y"), quarter, t]).astype(jnp.int32)
    grads_z, grads_y, *halves_of, done = first_grads_of(
        place, normed_all, branch_grad_all, joined_grad, mixed, first_all, joined_sums, unit_sums, small, row_sums
    )

    blocks = grads_z.reshape(4, 576, 512), grads_y.reshape(4, 512, 512)
    came = [
        axis_swap(v, axis, mask)
        for v, (axis, mask) in zip(halves_of, (("z", 1), ("z", 3), ("y", 1), ("y", 3)))
    ]
    sent = ring_next(one_sums, one_came, done, out_from1, out_from3)
    from1, from3 = ring_last(sent)
    came = axis_next(("z", "y"), blocks, came, sent[1])
    second_sent = small_call(rows_kernel, [((32, 2048), BF16)] * 4, [second_grads], scalars=me)
    second_came = exchange(*second_sent)
    grad_tokens, tokens_done = small_call(
        first_back_kernel,
        [((128, 2048), F32)],
        [part(one_own, (128, 2048), 0, 0), block_of(one_near, 0), from1, from3, tokens, middle_grad, small],
        token=True,
    )
    layer_out, out_done = small_call(
        output_kernel,
        [((128, 2048), BF16)],
        [part(out_own, (128, 2048), 0, 0), block_of(out_near, 0), out_from1, out_from3, middle, small],
        token=True,
    )

    terms_a, terms_b = axis_turn(*blocks, came, tokens_done, out_done, *second_came)
    first_sent = small_call(
        return_kernel,
        [((48, 1024), BF16)] * 4,
        [*terms_a, *terms_b],
        scalars=me,
    )

    grad_up, grad_down, place_done = small_call(
        functools.partial(place_kernel, (1024, 1024)),
        [((32, 4096), F32), ((32, 4096), F32)],
        second_came,
        scalars=me,
        token=True,
    )
    grad_qkv, grad_out, mine = small_call(
        functools.partial(place_kernel, (768, 256)),
        [((32, 3072), F32), ((32, 1024), F32), ((16, 256), F32)],
        exchange(*first_sent),
        place_done,
        scalars=me,
    )
    mine = mine + swap_x(mine, 1)
    vectors = lax.dynamic_slice(mine, (0, quarter * 32 + t * 16), (6, 16))
    joined_bias = lax.dynamic_slice(mine, (8 + xh, (c * 2 + t) * 48), (1, 48))
    unit_bias = lax.dynamic_slice(mine, (10 + xh, (c * 2 + t) * 64), (1, 64))

    return (
        layer_out,
        grad_tokens,
        vectors[4],
        vectors[5],
        grad_qkv,
        joined_bias[0],
        grad_out,
        vectors[0],
        vectors[1],
        vectors[2],
        grad_up,
        unit_bias[0],
        grad_down,
        vectors[3],
    )


def solution(mesh):
    fine = Mesh(mesh.devices.reshape(2, 4, 4, 2, 2), AXES)
    dp = ("xh", "z", "y", "c")
    rows, vec, mat = P(AXES, None), P(AXES), P(dp, "t")
    return jax.shard_map(
        body,
        mesh=fine,
        in_specs=(
            rows, P(dp, None), vec, vec, mat, vec, mat, vec, vec, vec, mat, vec, mat, vec, rows,
        ),
        out_specs=(
            rows, rows, vec, vec, mat, vec, mat, vec, vec, vec, mat, vec, mat, vec,
        ),
        check_vma=False,
    )
```

```python
import functools
import functools
import math

import jax
import jax.numpy as jnp
from jax import lax
from jax.experimental import pallas as pl
from jax.experimental.pallas import tpu as pltpu
from jax.sharding import Mesh
from jax.sharding import PartitionSpec as P

H = 16
HD = 128
PIECE = 64
EPS = 1e-05
GELU_COEF = math.sqrt(2.0 / math.pi)
SCALE = 1.0 / math.sqrt(HD)

AXES = ("xh", "z", "y", "c", "t")
RING = ("xh", "t")
PLANE = ("z", "y")
BF16 = jnp.bfloat16
F32 = jnp.float32


def gelu_tanh(values):
    return (
        0.5 * values * (1.0 + jnp.tanh(GELU_COEF * (values + 0.044715 * values * values * values)))
    )


def gelu_slope(values):
    square = values * values
    inner = jnp.tanh(GELU_COEF * (values + 0.044715 * values * square))
    return 0.5 * (1.0 + inner) + 0.5 * values * (1.0 - inner * inner) * GELU_COEF * (
        1.0 + 3.0 * 0.044715 * square
    )


def contract_rows(left_side, right_side):
    return lax.dot_general(
        left_side, right_side, (((0,), (0,)), ((), ())), preferred_element_type=F32
    )


def contract_cols(left_side, right_side):
    return lax.dot_general(
        left_side, right_side, (((1,), (1,)), ((), ())), preferred_element_type=F32
    )


def swap_x(v, mask):
    return lax.ppermute(v, RING, [(i, i ^ mask) for i in range(4)])


def swap_c(v):
    return lax.ppermute(v, "c", [(0, 1), (1, 0)])


ANYWHERE = pl.BlockSpec(memory_space=pl.ANY)
ENTIRE = pl.BlockSpec()
SCALARS = pl.BlockSpec(memory_space=pltpu.SMEM)


def far(*arrays):
    return [pltpu.with_memory_space_constraint(v, pltpu.HBM) for v in arrays]


def part(array, block, *index):
    return pltpu.with_memory_space_constraint(array, pltpu.HBM), pl.BlockSpec(block, lambda _: index)


def small_call(kernel, outs, operands, *others, scalars=None, token=False, large=2**18):
    first = [] if scalars is None else [scalars]
    outs = [*outs, ((8, 128), F32)] if token else outs
    operands = [v if isinstance(v, tuple) else (v, ENTIRE) for v in operands]

    def run(*refs):
        used = len(first) + len(operands)
        if token:
            *refs, done_ref = refs
            done_ref[...] = jnp.zeros_like(done_ref)
        kernel(*refs[:used], *refs[used + len(others) :])

    return pl.pallas_call(
        run,
        grid=(1,),
        in_specs=[SCALARS] * len(first) + [spec for _, spec in operands] + [ANYWHERE] * len(others),
        out_specs=[ENTIRE] * len(outs),
        out_shape=[
            (pltpu.HBM if math.prod(shape) * (2 if dtype == F32 else 1) > large else jax.ShapeDtypeStruct)(
                shape, dtype
            )
            for shape, dtype in outs
        ],
        compiler_params=pltpu.CompilerParams(vmem_limit_bytes=24 << 20),
        cost_estimate=pl.CostEstimate(flops=0, bytes_accessed=4 << 20, transcendentals=0),
    )(*first, *(v for v, _ in operands), *others)


def block_of(array, index):
    return array, pl.BlockSpec((128, 2048), lambda _: (index, 0))


def gate_kernel(*refs):
    pass


def joined(values, *others):
    return pl.pallas_call(
        gate_kernel,
        in_specs=[ANYWHERE] * (len(values) + len(others)),
        out_specs=[ANYWHERE] * len(values),
        out_shape=[pltpu.HBM(v.shape, v.dtype) for v in values],
        input_output_aliases={i: i for i in range(len(values))},
        cost_estimate=pl.CostEstimate(flops=0, bytes_accessed=0, transcendentals=0),
    )(*values, *others)


def split_kernel(one_ref, three_ref, low_ref, high_ref):
    half = low_ref.shape[0]
    low_ref[...] = three_ref[:half]
    high_ref[...] = one_ref[half:]


def pile_kernel(*refs):
    *pieces, out_ref = refs
    at = 0
    for piece in pieces:
        rows = piece.shape[0]
        out_ref[at : at + rows] = piece[...]
        at += rows


def gather_start(v):
    return swap_x(v, 1), swap_x(v, 3)


def gather_split(came, *others):
    rows, width = came[0].shape
    return small_call(split_kernel, [((rows // 2, width), BF16)] * 2, came, *others)


def gather_onward(onward):
    return swap_x(onward[0], 1), swap_x(onward[1], 3)


def gather_finish(v, came, opposite, *others):
    rows, width = v.shape
    pieces = [v, came[0], *opposite, came[1]]
    (own,) = small_call(pile_kernel, [((4 * rows, width), BF16)], pieces, *others)
    return own, swap_c(own)


def gather_group(v):
    came = gather_start(v)
    return gather_finish(v, came, gather_onward(gather_split(came)))


def add_low(*values):
    return sum(v.astype(F32) for v in values).astype(BF16)


def swap_cores(far):
    near, beyond = far
    return swap_c(beyond), swap_c(near)


def ring_two_kernel(own, beyond, low_ref, high_ref):
    two = add_low(own[...], beyond[...])
    half = low_ref.shape[0]
    low_ref[...] = two[:half]
    high_ref[...] = two[half:]


def ring_two(sums, *others):
    own, _, beyond = sums
    outs = [((64, 2048), BF16)] * 2
    ins = [part(own, (128, 2048), 2, 0), block_of(beyond, 0)]
    low, high, done = small_call(ring_two_kernel, outs, ins, *others, token=True)
    return (swap_x(low, 1), swap_x(high, 3)), done


def ring_next_kernel(own1, own3, near, beyond, add3_ref, add1_ref, s1_ref, s3_ref):
    half = add3_ref.shape[0]
    s3_ref[:half] = add_low(own3[:half], beyond[:half], add3_ref[...])
    s3_ref[half:] = add_low(own3[half:], beyond[half:])
    s1_ref[:half] = add_low(own1[:half], near[:half])
    s1_ref[half:] = add_low(own1[half:], near[half:], add1_ref[...])


def ring_next(sums, came, *others, large=2**18):
    own, near, beyond = sums
    own1, own3 = part(own, (128, 2048), 1, 0), part(own, (128, 2048), 3, 0)
    ins = [own1, own3, block_of(near, 1), block_of(beyond, 1), *came]
    return small_call(
        ring_next_kernel, [((128, 2048), BF16)] * 2, ins, *others, token=True, large=large
    )


def ring_last(sent):
    return swap_x(sent[0], 1), swap_x(sent[1], 3)


def axis_swap(v, axis, mask):
    return lax.ppermute(v, axis, [(i, i ^ mask) for i in range(4)])


def axis_next_kernel(a1, a3, add3_a, add1_a, b1, b3, add3_b, add1_b, *outs):
    for (one, three, add3, add1), (one_ref, three_ref) in (
        ((a1, a3, add3_a, add1_a), outs[:2]),
        ((b1, b3, add3_b, add1_b), outs[2:]),
    ):
        half = add3.shape[0]
        three_ref[:half] = add_low(three[0, :half], add3[...])
        three_ref[half:] = three[0, half:]
        one_ref[:half] = one[0, :half]
        one_ref[half:] = add_low(one[0, half:], add1[...])


def axis_next(axes, blocks, came, *others):
    a, b = blocks
    outs = [((a.shape[1], 512), BF16)] * 2 + [((b.shape[1], 512), BF16)] * 2
    pick = lambda v, i: part(v, (1, *v.shape[1:]), i, 0, 0)
    ins = [pick(a, 1), pick(a, 3), *came[:2], pick(b, 1), pick(b, 3), *came[2:]]
    one_a, three_a, one_b, three_b = small_call(axis_next_kernel, outs, ins, *others)
    return (
        axis_swap(one_a, axes[0], 1),
        axis_swap(three_a, axes[0], 3),
        axis_swap(one_b, axes[1], 1),
        axis_swap(three_b, axes[1], 3),
    )


def axis_turn_kernel(a_ref, a1, a3, b_ref, b1, b3, *outs):
    sum_a = add_low(a_ref[0], a1[...], a3[...]).reshape(4, 144, 512)
    sum_b = add_low(b_ref[0], b1[...], b3[...]).reshape(4, 128, 512)
    for i in range(4):
        outs[i][...] = sum_a[i]
        outs[4 + i][...] = sum_b[i]


def axis_turn(a, b, came, *others):
    ins = [part(a, (1, 576, 512), 0, 0, 0), *came[:2], part(b, (1, 512, 512), 0, 0, 0), *came[2:]]
    outs = [((144, 512), BF16)] * 4 + [((128, 512), BF16)] * 4
    own = small_call(axis_turn_kernel, outs, ins, *others)
    sum_a, sum_b = own[:4], own[4:]
    terms_a = [sum_a[0], *(axis_swap(sum_a[i], "y", i) for i in (2, 1, 3))]
    terms_b = [sum_b[0], *(axis_swap(sum_b[i], "z", i) for i in (2, 1, 3))]
    return terms_a, terms_b


def exchange(own, near, far, cross):
    return (
        own,
        swap_c(near),
        lax.ppermute(far, "xh", [(0, 1), (1, 0)]),
        lax.ppermute(cross, ("xh", "c"), [(i, 3 - i) for i in range(4)]),
    )


def spread_kernel(me_ref, *refs):
    parts, outs = refs[:-4], refs[-4:]
    for other, out_ref in enumerate(outs):
        quarter = me_ref[0] ^ other
        at = 0
        for part_ref in parts:
            if part_ref.shape[0] == 32:
                width = part_ref.shape[1] // 4
                start = pl.multiple_of(quarter * width, 128)
                out_ref[:32, at : at + width] = part_ref[:, pl.ds(start, width)]
                at += width
            else:
                out_ref[32:] = part_ref[...]


def collect_kernel(me_ref, *refs):
    *came, out_ref = refs
    for other, part_ref in enumerate(came):
        start = pl.multiple_of((me_ref[0] ^ other) * 32, 32)
        out_ref[pl.ds(start, 32)] = part_ref[:32]
    if out_ref.shape[0] > 128:
        out_ref[128:] = add_low(*(part_ref[32:] for part_ref in came))


def spread_columns(me, parts, *others, extra=None):
    below = 0 if extra is None else 16
    width = sum(p.shape[1] for p in parts) // 4
    ins = far(*parts) if extra is None else [*far(*parts), extra]
    sent = small_call(spread_kernel, [((32 + below, width), BF16)] * 4, ins, *others, scalars=me)
    (rows,) = small_call(
        collect_kernel, [((128 + below, width), BF16)], exchange(*sent), scalars=me
    )
    return rows


def rows_kernel(me_ref, rows_ref, *outs):
    for other, out_ref in enumerate(outs):
        start = pl.multiple_of((me_ref[0] ^ other) * 32, 32)
        out_ref[...] = rows_ref[pl.ds(start, 32)]


def return_kernel(me_ref, *refs):
    terms, outs = refs[:8], refs[8:]
    sum_a = add_low(*(v[...] for v in terms[:4]))
    sum_b = add_low(*(v[...] for v in terms[4:]))
    for at in range(4):
        rows = slice(at * 32, at * 32 + 32)

        for other, out_ref in enumerate(outs):

            @pl.when(me_ref[0] ^ other == at)
            def _():
                out_ref[:32, :512] = sum_a[rows]
                out_ref[:32, 512:] = sum_b[rows]

    for out_ref in outs:
        out_ref[32:, :512] = sum_a[128:]
        out_ref[32:, 512:] = jnp.zeros((16, 512), BF16)


def place_kernel(widths, me_ref, *refs):
    came, outs = refs[:4], refs[4:]
    for other, part_ref in enumerate(came):
        quarter = me_ref[0] ^ other
        at = 0
        for ref, width in zip(outs, widths):
            start = pl.multiple_of(quarter * width, 128)
            ref[:, pl.ds(start, width)] = part_ref[:32, at : at + width].astype(F32)
            at += width
    if len(outs) > len(widths):
        outs[-1][...] = sum(part_ref[32:, :256].astype(F32) for part_ref in came)


def two_pieces(v):
    high = lax.reduce_precision(v, 8, 7)
    return jnp.stack([high, v - high]).astype(BF16)


def small_block(vectors, joined_bias, unit_bias, starts, xh, c, t):
    flat = jnp.concatenate([*vectors, joined_bias, unit_bias])
    other = swap_x(flat, 1)
    pair = jnp.where(t == 0, jnp.stack([flat, other]), jnp.stack([other, flat]))
    pieces = two_pieces(pair)
    mine = (jnp.arange(4) == xh * 2 + c).astype(BF16)
    rows = pieces[:, :, :96].reshape(2, 2, 6, 16).transpose(2, 0, 1, 3).reshape(6, 2, 1, 32)
    rows = (rows * mine[:, None]).reshape(6, 256)
    joined = (pieces[:, :, 96:144].reshape(2, 1, 96) * mine[:, None]).reshape(2, 384)
    unit = (pieces[:, :, 144:].reshape(2, 1, 128) * mine[:, None]).reshape(2, 512)
    starts = (starts.astype(BF16) * mine[:, None]).reshape(1, 8)
    wide = lambda v: jnp.pad(v, ((0, 0), (0, 1024 - v.shape[1])))
    return jnp.concatenate(
        [wide(rows), wide(joined), wide(unit), wide(starts), jnp.zeros((5, 1024), BF16)], axis=0
    )


def low_half(rows):
    return lax.broadcasted_iota(jnp.int32, (rows, 128), 1) < 64


def store_plane(ref, values):
    low = low_half(values.shape[0])
    for j in range(8):
        a = values[:, j * 128 : j * 128 + 128]
        b = values[:, 1024 + j * 128 : 1024 + j * 128 + 128]
        at = j * 256
        ref[:, at : at + 128] = jnp.where(low, a, pltpu.roll(b, 64, 1)).astype(ref.dtype)
        ref[:, at + 128 : at + 256] = jnp.where(low, pltpu.roll(a, 64, 1), b).astype(ref.dtype)


def natural(values):
    low = low_half(values.shape[0])
    first, second = [], []
    for j in range(8):
        a = values[:, j * 256 : j * 256 + 128]
        b = values[:, j * 256 + 128 : j * 256 + 256]
        first.append(jnp.where(low, a, pltpu.roll(b, 64, 1)))
        second.append(jnp.where(low, pltpu.roll(a, 64, 1), b))
    return jnp.concatenate(first + second, axis=1)


def total_of(refs):
    return natural(sum(r[...].astype(F32) for r in refs))


def row_stats(values):
    centre = values - jnp.mean(values, axis=-1, keepdims=True)
    spread = jnp.mean(centre * centre, axis=-1, keepdims=True)
    return centre, lax.rsqrt(spread + EPS)


def norm_back(values, gain, upstream):
    centre, scale = row_stats(values)
    vhat = centre * scale
    e = upstream * gain
    dv = scale * (
        e - jnp.mean(e, axis=-1, keepdims=True) - vhat * jnp.mean(e * vhat, axis=-1, keepdims=True)
    )
    return dv, vhat


def first_norm_kernel(x_ref, *outs):
    n_ref, done_ref = outs[-2:]
    done_ref[...] = jnp.zeros_like(done_ref)
    centre, scale = row_stats(x_ref[...].astype(F32))
    store_plane(n_ref, centre * scale)


def middle_kernel(t0, t1, t2, t3, x_ref, small_ref, mid_ref, n_ref):
    small = natural(small_ref[...])
    middle = x_ref[...].astype(F32) + (total_of((t0, t1, t2, t3)) + small[2:3])
    mid_ref[...] = middle
    centre, scale = row_stats(middle)
    store_plane(n_ref, centre * scale * small[3:4] + small[4:5])


def second_back_kernel(t0, t1, t2, t3, mid_ref, cot_ref, small_ref, dh_ref, low_ref, sum_ref):
    small = natural(small_ref[...])
    upstream = total_of((t0, t1, t2, t3))
    dv, vhat = norm_back(mid_ref[...], small[3:4], upstream)
    final = cot_ref[...].astype(F32)
    dh = final + dv
    dh_ref[...] = dh
    store_plane(low_ref, dh)
    total = lambda v: jnp.sum(v, axis=0, keepdims=True)
    store_plane(
        sum_ref,
        jnp.concatenate(
            [total(dh), total(upstream * vhat), total(upstream), total(final), jnp.zeros((4, 2048), F32)],
            axis=0,
        ),
    )


def first_back_kernel(t0, t1, t2, t3, x_ref, dh_ref, small_ref, g_ref):
    small = natural(small_ref[...])
    dv, _ = norm_back(x_ref[...].astype(F32), small[0:1], total_of((t0, t1, t2, t3)))
    g_ref[...] = dh_ref[...] + dv


def output_kernel(t0, t1, t2, t3, mid_ref, small_ref, o_ref):
    small = natural(small_ref[...])
    o_ref[...] = (mid_ref[...] + (total_of((t0, t1, t2, t3)) + small[5:6])).astype(BF16)


def plane_kernel(x_ref, o_ref):
    store_plane(o_ref, x_ref[...].astype(F32))


PARAMS = pltpu.CompilerParams(vmem_limit_bytes=48 << 20)


def cost(flops, mebibytes):
    return pl.CostEstimate(flops=int(flops), bytes_accessed=int(mebibytes * 2**20), transcendentals=0)


def whole_call(kernel, outs, *operands):
    return pl.pallas_call(
        kernel, out_shape=outs, compiler_params=PARAMS, cost_estimate=cost(0, 4)
    )(*operands)


def row_block(width):
    return pl.BlockSpec((256, width), lambda i: (i, 0))


def whole(*shape):
    return pl.BlockSpec(shape, lambda i: (0,) * len(shape))


def halves(*block):
    tail = (0,) * (len(block) - 1)
    return [
        pl.BlockSpec(block, lambda i: (jnp.minimum(i, 1), *tail)),
        pl.BlockSpec(block, lambda i: (jnp.maximum(i - 2, 0), *tail)),
    ]


def pick(own_ref, other_ref):
    return jnp.where(pl.program_id(0) < 2, own_ref[...], other_ref[...])


def contract_both(own, other, right):
    half = right.shape[0] // 2
    return contract_rows(own, right[:half]) + contract_rows(other, right[half:])


def like(rows, dtype):
    return jax.ShapeDtypeStruct((rows, 2048), dtype)


def first_norm(x, half=None):
    at = 0 if half is None else 2
    return pl.pallas_call(
        first_norm_kernel,
        grid=(2,),
        in_specs=[row_block(2048)] + [ANYWHERE] * (half is not None),
        out_specs=[pl.BlockSpec((256, 2048), lambda i: (i + at, 0)), whole(8, 128)],
        out_shape=[pltpu.HBM((1024, 2048), F32), jax.ShapeDtypeStruct((8, 128), F32)],
        input_output_aliases={} if half is None else {1: 0},
        compiler_params=PARAMS,
        cost_estimate=cost(0, 8),
    )(*far(x), *(() if half is None else (half,)))


def up_grads_kernel(own_ref, other_ref, du_ref, out_ref, done_ref):
    done_ref[...] = jnp.zeros_like(done_ref)
    out_ref[...] = contract_both(own_ref[...], other_ref[...], du_ref[...]).astype(BF16)


def down_grads_kernel(_, own_ref, other_ref, a_ref, out_ref, done_ref):
    done_ref[...] = jnp.zeros_like(done_ref)
    out_ref[...] = contract_both(own_ref[...], other_ref[...], a_ref[...]).astype(BF16)


def up_grads(n, du):
    rows, width = du.shape
    return pl.pallas_call(
        up_grads_kernel,
        grid=(4,),
        in_specs=[pl.BlockSpec((512, 512), lambda i: (0, i))] * 2 + [whole(rows, width)],
        out_specs=[pl.BlockSpec((512, width), lambda i: (i, 0)), whole(8, 128)],
        out_shape=[
            pltpu.HBM((2048, 2 * width), BF16),
            jax.ShapeDtypeStruct((8, 128), F32),
        ],
        compiler_params=PARAMS,
        cost_estimate=cost(5e9, 10),
    )(*far(n[0]), n[1], *far(du))


def down_grads(left, cot, a):
    rows, width = a.shape
    return pl.pallas_call(
        down_grads_kernel,
        grid=(4,),
        in_specs=[ANYWHERE]
        + [pl.BlockSpec((512, 512), lambda i: (0, i))] * 2
        + [whole(rows, width)],
        out_specs=[pl.BlockSpec((512, width), lambda i: (i, 1)), whole(8, 128)],
        out_shape=[
            pltpu.HBM(left.shape, BF16),
            jax.ShapeDtypeStruct((8, 128), F32),
        ],
        input_output_aliases={0: 0},
        compiler_params=PARAMS,
        cost_estimate=cost(5e9, 10),
    )(left, *far(*cot, a))


def first_grads_kernel(
    place_ref, n_ref, own_ref, other_ref, df_ref, o_ref, w_ref, total_ref, unit_ref, small_ref, sums_ref,
    a_ref, b_ref, al_ref, ah_ref, bl_ref, bh_ref, done_ref
):
    done_ref[...] = jnp.zeros_like(done_ref)
    y = place_ref[1]
    joined = contract_rows(n_ref[...], df_ref[...])
    weight = w_ref[...].reshape(512, 768)
    weighted = joined * weight.astype(F32)
    weighted = sum(weighted[:, j * 128 : j * 128 + 128] for j in range(6))
    ones = jnp.ones((8, 128), BF16)
    high = weighted.astype(BF16)
    weighted = contract_cols(ones, high) + contract_cols(ones, (weighted - high.astype(F32)).astype(BF16))
    shift = contract_cols(total_ref[...].astype(BF16), weight)[0:1]
    gain = (weighted[0:1] - small_ref[1:2] * shift) / small_ref[0:1]
    sums = jnp.concatenate([sums_ref[:4], gain, shift, jnp.zeros((2, 512), F32)], axis=0)
    z = pl.program_id(0)
    z_to = z ^ place_ref[0]
    here = (z == place_ref[2]).astype(F32)
    row = lax.broadcasted_iota(jnp.int32, (8, 256), 0)
    row_of = lambda v, at: jnp.where(row == at, v[0:1, :256] * here, 0.0)
    joined_total = total_ref[...]
    joined = joined.astype(BF16)
    out = contract_both(own_ref[...], other_ref[...], o_ref[...]).astype(BF16)
    for i in range(4):
        rows = slice(i * 128, i * 128 + 128)
        mine = pltpu.roll(joined_total, 768 - i * 192, 1) if i else joined_total
        biases = row_of(mine, place_ref[3]) + row_of(
            unit_ref[:, i * 256 : i * 256 + 256], 2 + place_ref[3]
        )
        low = jnp.concatenate([sums[:, rows], jnp.zeros((8, 384), F32)], axis=1)
        high = jnp.concatenate([biases, jnp.zeros((8, 256), F32)], axis=1)
        below = jnp.concatenate([low, high], axis=0).astype(BF16)
        y_to = i ^ y
        a_ref[0, y_to, :128] = joined[rows, :512]
        a_ref[0, y_to, 128:] = below
        b_ref[y_to, 0, :, :256] = joined[rows, 512:]
        b_ref[y_to, 0, :, 256:] = out[rows]

        for half, (low_ref, high_ref) in enumerate(((al_ref, bl_ref), (ah_ref, bh_ref))):

            @pl.when((z_to == 2) & (y_to // 2 == half))
            def _():
                at = pl.multiple_of((y_to % 2) * 144, 16)
                low_ref[pl.ds(at, 128)] = joined[rows, :512]
                low_ref[pl.ds(at + 128, 16)] = below

            @pl.when((y_to == 2) & (z_to // 2 == half))
            def _():
                at = pl.multiple_of((z_to % 2) * 128, 128)
                high_ref[pl.ds(at, 128), :256] = joined[rows, 512:]
                high_ref[pl.ds(at, 128), 256:] = out[rows]


def first_grads_of(place, n, dh, df, o, first_all, total, unit_total, small, sums):
    rows = n.shape[0]
    return pl.pallas_call(
        first_grads_kernel,
        grid_spec=pltpu.PrefetchScalarGridSpec(
            num_scalar_prefetch=1,
            grid=(4,),
            in_specs=[
                pl.BlockSpec((rows, 512), lambda i, p: (0, i)),
                pl.BlockSpec((512, 512), lambda i, p: (0, i)),
                pl.BlockSpec((512, 512), lambda i, p: (0, i)),
                pl.BlockSpec((rows, 768), lambda i, p: (0, 0)),
                pl.BlockSpec((rows, 256), lambda i, p: (0, 0)),
                pl.BlockSpec((4, 128, 768), lambda i, p: (i, 0, 0)),
                pl.BlockSpec((8, 768), lambda i, p: (0, 0)),
                pl.BlockSpec((8, 1024), lambda i, p: (0, 0)),
                pl.BlockSpec((8, 512), lambda i, p: (0, i)),
                pl.BlockSpec((8, 512), lambda i, p: (0, i)),
            ],
            out_specs=[
                pl.BlockSpec((1, 4, 144, 512), lambda i, p: (i ^ p[0], 0, 0, 0)),
                pl.BlockSpec((4, 1, 128, 512), lambda i, p: (0, i ^ p[0], 0, 0)),
                *(pl.BlockSpec((v, 512), lambda i, p: (0, 0)) for v in (288, 288, 256, 256)),
                pl.BlockSpec((8, 128), lambda i, p: (0, 0)),
            ],
        ),
        out_shape=[
            pltpu.HBM((4, 4, 144, 512), BF16),
            pltpu.HBM((4, 4, 128, 512), BF16),
            *(jax.ShapeDtypeStruct((v, 512), BF16) for v in (288, 288, 256, 256)),
            jax.ShapeDtypeStruct((8, 128), F32),
        ],
        compiler_params=PARAMS,
        cost_estimate=cost(40e9, 16),
    )(place, *far(n, *dh, df, o, first_all), total, unit_total, small, sums)


def bias_of(info_ref, seq):
    flip_half = info_ref[8]
    row = lax.broadcasted_iota(jnp.int32, (256, 1), 0) ^ (flip_half * 128)
    col = lax.broadcasted_iota(jnp.int32, (1, 256), 1) ^ (flip_half * 128)
    allowed = col <= row
    place = (info_ref[9] ^ (seq % 2)) * 2 + (info_ref[10] ^ (seq // 2))
    for p in range(2):
        start = info_ref[place * 2 + p]
        in_row = (row >= start) & (row < start + PIECE)
        in_col = (col >= start) & (col < start + PIECE)
        allowed = allowed | (in_row & in_col)
    return jnp.abs(row - col).astype(F32), allowed


def softmax_of(slope, distance, allowed, query, keys):
    s = contract_cols(query, keys) * SCALE - slope * distance
    s = jnp.where(allowed, s, -1e30)
    e = jnp.exp(s - jnp.max(s, axis=-1, keepdims=True))
    return e * (1.0 / jnp.sum(e, axis=-1, keepdims=True))


def store_partial(out_refs, values):
    own_ref, near_ref, beyond_ref = out_refs
    step = pl.program_id(0)
    values = values.astype(BF16)

    @pl.when(step < 2)
    def _():
        own_ref[...] = values

    @pl.when(step == 2)
    def _():
        near_ref[...] = values

    @pl.when(step == 3)
    def _():
        beyond_ref[...] = values


PARTIAL_SPECS = [
    pl.BlockSpec((256, 2048), lambda i: (jnp.minimum(i, 1), 0)),
    pl.BlockSpec((256, 2048), lambda i: (0, 0)),
    pl.BlockSpec((256, 2048), lambda i: (0, 0)),
]
PARTIAL = [pltpu.HBM((rows, 2048), BF16) for rows in (512, 256, 256)]


def forward_kernel(
    info_ref, slopes_ref, v_ref, rows_ref, w_ref, _, n_ref, f_ref, o_ref, done_ref, small_ref, unit_ref,
    *out_refs
):
    seq = pl.program_id(0)
    *out_refs, bias_ref = out_refs

    @pl.when(seq == 0)
    def _():
        done_ref[...] = jnp.zeros_like(done_ref)
        for place in range(16):
            rows = rows_ref[place, :, :256].astype(F32)
            small_ref[:, place * 128 : place * 128 + 128] = (rows[:, :128] + rows[:, 128:])[:8]
        quarter, t = info_ref[9] * 2 + info_ref[10], info_ref[8]
        lane = lax.broadcasted_iota(jnp.int32, (1, 1024), 1)
        for first, width, ref in ((6, 192, bias_ref), (8, 256, unit_ref)):
            total = jnp.zeros((1, 1024), F32)
            for y in range(4):
                rows = rows_ref[quarter * 4 + y].astype(F32)
                rows = pltpu.roll(rows, (y * width - t * width + 1024) % 1024, 1)
                rows = rows[first : first + 1] + rows[first + 1 : first + 2]
                here = (lane >= y * width) & (lane < (y + 1) * width)
                total = total + jnp.where(here, rows, 0.0)
            ref[...] = jnp.broadcast_to(total[:, : ref.shape[1]], ref.shape)

    n = (v_ref[...] * small_ref[0:1] + small_ref[1:2]).astype(BF16)
    n_ref[...] = n
    weight = w_ref[...].reshape(2048, 1024)
    f = (jnp.dot(n, weight[:, :768], preferred_element_type=F32) + bias_ref[0:1]).astype(BF16)
    f_ref[...] = f
    distance, allowed = bias_of(info_ref, seq)
    mixed = []
    for head in range(2):
        q, k, v = (f[:, (head * 3 + i) * HD : (head * 3 + i + 1) * HD] for i in range(3))
        prob = softmax_of(slopes_ref[head], distance, allowed, q, k).astype(BF16)
        mixed.append(jnp.dot(prob, v, preferred_element_type=F32).astype(BF16))
    mixed = jnp.concatenate(mixed, axis=1)
    o_ref[...] = mixed
    store_partial(out_refs, contract_cols(mixed, weight[:, 768:]))


def backward_kernel(
    info_ref, slopes_ref, f_ref, own_ref, other_ref, w_ref, _, df_ref, sum_ref, *out_refs
):
    seq = pl.program_id(0)

    @pl.when(seq == 0)
    def _():
        sum_ref[...] = jnp.zeros_like(sum_ref)

    dh = pick(own_ref, other_ref)
    weight = w_ref[...].reshape(2048, 1024)
    grad = jnp.dot(
        dh, weight[:, 768:], preferred_element_type=F32
    ).astype(BF16)
    distance, allowed = bias_of(info_ref, seq)
    for head in range(2):
        base = head * 3 * HD
        q = f_ref[:, base : base + HD]
        k = f_ref[:, base + HD : base + 2 * HD]
        v = f_ref[:, base + 2 * HD : base + 3 * HD]
        g = grad[:, head * HD : (head + 1) * HD]
        prob = softmax_of(slopes_ref[head], distance, allowed, q, k)
        dp = contract_cols(g, v)
        row_dot = jnp.sum(prob * dp, axis=-1, keepdims=True)
        ds = (prob * (dp - row_dot) * SCALE).astype(BF16)
        dq = jnp.dot(ds, k, preferred_element_type=F32)
        dk = contract_rows(ds, q)
        dv = contract_rows(prob.astype(BF16), g)
        for i, part in enumerate((dq, dk, dv)):
            at = base + i * HD
            df_ref[:, at : at + HD] = part.astype(BF16)
            sum_ref[0:1, at : at + HD] += jnp.sum(part, axis=0, keepdims=True)
    store_partial(out_refs, contract_cols(df_ref[...], weight[:, :768]))


def forward_attention(info, slopes, vhat, first_all, other):
    rows = 1024
    return pl.pallas_call(
        forward_kernel,
        grid=(rows // 256,),
        in_specs=[
            SCALARS,
            SCALARS,
            row_block(2048),
            pl.BlockSpec((16, 16, 1024), lambda i: (0, 8, 0)),
            whole(16, 128, 1024),
            ANYWHERE,
        ],
        out_specs=[
            row_block(2048),
            row_block(768),
            row_block(256),
            whole(8, 128),
            whole(8, 2048),
            whole(8, 1024),
            *PARTIAL_SPECS,
        ],
        out_shape=[
            pltpu.HBM((rows, 2048), BF16),
            pltpu.HBM((rows, 768), BF16),
            pltpu.HBM((rows, 256), BF16),
            jax.ShapeDtypeStruct((8, 128), F32),
            like(8, F32),
            jax.ShapeDtypeStruct((8, 1024), F32),
            *PARTIAL,
        ],
        scratch_shapes=[pltpu.VMEM((8, 768), F32)],
        compiler_params=PARAMS,
        cost_estimate=cost(10e9, 24),
    )(info, slopes, *far(vhat, first_all, first_all), other)


def backward_attention(info, slopes, f, dh, first_all, other):
    rows = f.shape[0]
    return pl.pallas_call(
        backward_kernel,
        grid=(rows // 256,),
        in_specs=[
            SCALARS,
            SCALARS,
            row_block(768),
            *halves(256, 2048),
            whole(16, 128, 1024),
            ANYWHERE,
        ],
        out_specs=[row_block(768), whole(8, 768), *PARTIAL_SPECS],
        out_shape=[
            pltpu.HBM((rows, 768), BF16),
            jax.ShapeDtypeStruct((8, 768), F32),
            *PARTIAL,
        ],
        compiler_params=PARAMS,
        cost_estimate=cost(86e9, 10),
    )(info, slopes, *far(f, dh[0]), dh[1], *far(first_all), other)


def unit_kernel(n0_ref, n1_ref, c0_ref, c1_ref, w_ref, bias_ref, a_ref, du_ref, sum_ref, *out_refs):
    @pl.when(pl.program_id(0) == 0)
    def _():
        sum_ref[...] = jnp.zeros_like(sum_ref)

    n, cot = pick(n0_ref, n1_ref), pick(c0_ref, c1_ref)
    w_up, w_down = w_ref[:, :1024], w_ref[:, 1024:]
    u = jnp.dot(n, w_up, preferred_element_type=F32) + bias_ref[0:1]
    da = jnp.dot(cot, w_down, preferred_element_type=F32)
    a_ref[...] = gelu_tanh(u).astype(BF16)
    du = da * gelu_slope(u)
    sum_ref[0:1] += jnp.sum(du, axis=0, keepdims=True)
    du = du.astype(BF16)
    du_ref[...] = du
    total = contract_cols(du, w_up)
    store_partial(out_refs, total)


def units(n, cot, second_all, bias):
    rows = 1024
    return pl.pallas_call(
        unit_kernel,
        grid=(rows // 256,),
        in_specs=[
            *halves(256, 2048),
            *halves(256, 2048),
            whole(2048, 2048),
            whole(8, 1024),
        ],
        out_specs=[row_block(1024), row_block(1024), whole(8, 1024), *PARTIAL_SPECS],
        out_shape=[
            pltpu.HBM((rows, 1024), BF16),
            pltpu.HBM((rows, 1024), BF16),
            jax.ShapeDtypeStruct((8, 1024), F32),
            *PARTIAL,
        ],
        compiler_params=PARAMS,
        cost_estimate=cost(18e9, 24),
    )(*far(n[0]), n[1], *far(*cot, second_all), bias)


def unit_output_kernel(a_ref, w_ref, *out_refs):
    *out_refs, done_ref = out_refs
    done_ref[...] = jnp.zeros_like(done_ref)
    store_partial(out_refs, contract_cols(a_ref[...], w_ref[...]))


def unit_output(a, second_all):
    rows = a.shape[0]
    return pl.pallas_call(
        unit_output_kernel,
        grid=(rows // 256,),
        in_specs=[row_block(1024), pl.BlockSpec((2048, 1024), lambda i: (0, 1))],
        out_specs=[*PARTIAL_SPECS, whole(8, 128)],
        out_shape=[*PARTIAL, jax.ShapeDtypeStruct((8, 128), F32)],
        compiler_params=PARAMS,
        cost_estimate=cost(6e9, 12),
    )(*far(a, second_all))


def body(
    tokens,
    piece_starts,
    ln1_gain,
    ln1_bias,
    qkv_weight,
    qkv_bias,
    out_weight,
    out_bias,
    ln2_gain,
    ln2_bias,
    up_weight,
    up_bias,
    down_weight,
    down_bias,
    cotangent,
):
    xh, c, t = lax.axis_index("xh"), lax.axis_index("c"), lax.axis_index("t")
    quarter = xh * 2 + c

    me = quarter.reshape(1).astype(jnp.int32)
    small_own = small_block(
        (ln1_gain, ln1_bias, out_bias, ln2_gain, ln2_bias, down_bias), qkv_bias, up_bias, piece_starts, xh, c, t
    )
    first_rows = spread_columns(me, [qkv_weight, out_weight], extra=small_own)
    first_all = lax.all_gather(first_rows, PLANE, axis=0)
    second_rows = spread_columns(me, [up_weight, down_weight])
    second_all = lax.all_gather(second_rows, PLANE, axis=0, tiled=True)

    starts = first_rows[138, :8].astype(jnp.int32)
    info = jnp.concatenate([starts, jnp.stack([t, xh, c]).astype(jnp.int32)])
    head_ids = t * 8 + quarter * 2 + jnp.arange(2, dtype=jnp.int32)
    slopes = jnp.exp2(-8.0 * (head_ids.astype(F32) + 1.0) / H)

    came = gather_start(tokens)
    onward = gather_split(came, second_rows)
    tokens_all = gather_finish(tokens, came, gather_onward(onward))
    cot_plane = whole_call(plane_kernel, like(128, BF16), cotangent)
    came = gather_start(cot_plane)
    vhat, done = first_norm(tokens_all[1], first_norm(tokens_all[0])[0])
    onward = gather_split(came, done)
    opposite = gather_onward(onward)
    normed_all, f, mixed, done, small, bias_up, own, *other_core = forward_attention(
        info, slopes, vhat, first_all, onward[1]
    )
    cot_all = gather_finish(cot_plane, came, opposite, done)
    beyond, near = swap_cores(joined(other_core, cot_all[0]))
    sums = own, near, beyond
    from1, from3 = ring_last(ring_next(sums, ring_two(sums)[0]))
    middle, normed_two = small_call(
        middle_kernel,
        [((128, 2048), F32), ((128, 2048), BF16)],
        [part(own, (128, 2048), 0, 0), block_of(near, 0), from1, from3, tokens, small],
    )
    normed_two_all = gather_group(normed_two)
    active, hidden_grad, unit_sums, own, *other_core = units(normed_two_all, cot_all, second_all, bias_up)

    beyond, near = swap_cores(other_core)
    sums = own, near, beyond
    came, _ = ring_two(sums)
    second_out, done = up_grads(normed_two_all, hidden_grad)
    from1, from3 = ring_last(ring_next(sums, came, done))
    second_out, done = down_grads(second_out, cot_all, active)
    second_grads = lax.psum_scatter(second_out, PLANE, scatter_dimension=0, tiled=True)
    middle_grad, branch_grad, row_sums = small_call(
        second_back_kernel,
        [((128, 2048), F32), ((128, 2048), BF16), ((8, 2048), F32)],
        [part(own, (128, 2048), 0, 0), block_of(near, 0), from1, from3, middle, cotangent, small],
        done,
    )
    came = gather_start(branch_grad)
    out_own, *out_far, done = unit_output(active, second_all)
    onward = gather_split(came, done)
    branch_grad_all = gather_finish(branch_grad, came, gather_onward(onward))
    out_beyond, out_near = swap_cores(out_far)
    out_sums = out_own, out_near, out_beyond
    out_came, out_ready = ring_two(out_sums)

    joined_grad, joined_sums, one_own, *one_far = backward_attention(
        info, slopes, f, branch_grad_all, first_all, out_ready
    )
    out_sent = ring_next(out_sums, out_came, joined_sums, large=2**17)
    out_from1, out_from3 = ring_last(out_sent)
    one_beyond, one_near = swap_cores(joined(one_far, out_sent[1]))
    one_sums = one_own, one_near, one_beyond
    one_came, _ = ring_two(one_sums)
    place = jnp.stack([lax.axis_index("z"), lax.axis_index("y"), quarter, t]).astype(jnp.int32)
    grads_z, grads_y, *halves_of, done = first_grads_of(
        place, normed_all, branch_grad_all, joined_grad, mixed, first_all, joined_sums, unit_sums, small, row_sums
    )

    blocks = grads_z.reshape(4, 576, 512), grads_y.reshape(4, 512, 512)
    came = [
        axis_swap(v, axis, mask)
        for v, (axis, mask) in zip(halves_of, (("z", 1), ("z", 3), ("y", 1), ("y", 3)))
    ]
    sent = ring_next(one_sums, one_came, done, out_from1, out_from3)
    from1, from3 = ring_last(sent)
    came = axis_next(("z", "y"), blocks, came, sent[2])
    second_sent = small_call(rows_kernel, [((32, 2048), BF16)] * 4, [second_grads], scalars=me)
    second_came = exchange(*second_sent)
    grad_tokens, tokens_done = small_call(
        first_back_kernel,
        [((128, 2048), F32)],
        [part(one_own, (128, 2048), 0, 0), block_of(one_near, 0), from1, from3, tokens, middle_grad, small],
        token=True,
    )
    layer_out, out_done = small_call(
        output_kernel,
        [((128, 2048), BF16)],
        [part(out_own, (128, 2048), 0, 0), block_of(out_near, 0), out_from1, out_from3, middle, small],
        token=True,
    )

    terms_a, terms_b = axis_turn(*blocks, came, from1, from3, *second_came)
    first_sent = small_call(
        return_kernel,
        [((48, 1024), BF16)] * 4,
        [*terms_a, *terms_b],
        tokens_done,
        out_done,
        scalars=me,
    )

    grad_up, grad_down, place_done = small_call(
        functools.partial(place_kernel, (1024, 1024)),
        [((32, 4096), F32), ((32, 4096), F32)],
        second_came,
        scalars=me,
        token=True,
    )
    grad_qkv, grad_out, mine = small_call(
        functools.partial(place_kernel, (768, 256)),
        [((32, 3072), F32), ((32, 1024), F32), ((16, 256), F32)],
        exchange(*first_sent),
        place_done,
        scalars=me,
    )
    mine = mine + swap_x(mine, 1)
    vectors = lax.dynamic_slice(mine, (0, quarter * 32 + t * 16), (6, 16))
    joined_bias = lax.dynamic_slice(mine, (8 + xh, (c * 2 + t) * 48), (1, 48))
    unit_bias = lax.dynamic_slice(mine, (10 + xh, (c * 2 + t) * 64), (1, 64))

    return (
        layer_out,
        grad_tokens,
        vectors[4],
        vectors[5],
        grad_qkv,
        joined_bias[0],
        grad_out,
        vectors[0],
        vectors[1],
        vectors[2],
        grad_up,
        unit_bias[0],
        grad_down,
        vectors[3],
    )


def solution(mesh):
    fine = Mesh(mesh.devices.reshape(2, 4, 4, 2, 2), AXES)
    dp = ("xh", "z", "y", "c")
    rows, vec, mat = P(AXES, None), P(AXES), P(dp, "t")
    return jax.shard_map(
        body,
        mesh=fine,
        in_specs=(
            rows, P(dp, None), vec, vec, mat, vec, mat, vec, vec, vec, mat, vec, mat, vec, rows,
        ),
        out_specs=(
            rows, rows, vec, vec, mat, vec, mat, vec, vec, vec, mat, vec, mat, vec,
        ),
        check_vma=False,
    )
```

```python
import functools
import functools
import math

import jax
import jax.numpy as jnp
from jax import lax
from jax.experimental import pallas as pl
from jax.experimental.pallas import tpu as pltpu
from jax.sharding import Mesh
from jax.sharding import PartitionSpec as P

H = 16
HD = 128
PIECE = 64
EPS = 1e-05
GELU_COEF = math.sqrt(2.0 / math.pi)
SCALE = 1.0 / math.sqrt(HD)

AXES = ("xh", "z", "y", "c", "t")
RING = ("xh", "t")
PLANE = ("z", "y")
BF16 = jnp.bfloat16
F32 = jnp.float32


def gelu_tanh(values):
    return (
        0.5 * values * (1.0 + jnp.tanh(GELU_COEF * (values + 0.044715 * values * values * values)))
    )


def gelu_slope(values):
    square = values * values
    inner = jnp.tanh(GELU_COEF * (values + 0.044715 * values * square))
    return 0.5 * (1.0 + inner) + 0.5 * values * (1.0 - inner * inner) * GELU_COEF * (
        1.0 + 3.0 * 0.044715 * square
    )


def contract_rows(left_side, right_side):
    return lax.dot_general(
        left_side, right_side, (((0,), (0,)), ((), ())), preferred_element_type=F32
    )


def contract_cols(left_side, right_side):
    return lax.dot_general(
        left_side, right_side, (((1,), (1,)), ((), ())), preferred_element_type=F32
    )


def swap_x(v, mask):
    return lax.ppermute(v, RING, [(i, i ^ mask) for i in range(4)])


def swap_c(v):
    return lax.ppermute(v, "c", [(0, 1), (1, 0)])


ANYWHERE = pl.BlockSpec(memory_space=pl.ANY)
ENTIRE = pl.BlockSpec()
SCALARS = pl.BlockSpec(memory_space=pltpu.SMEM)


def far(*arrays):
    return [pltpu.with_memory_space_constraint(v, pltpu.HBM) for v in arrays]


def part(array, block, *index):
    return pltpu.with_memory_space_constraint(array, pltpu.HBM), pl.BlockSpec(block, lambda _: index)


def small_call(kernel, outs, operands, *others, scalars=None, token=False, large=2**18):
    first = [] if scalars is None else [scalars]
    outs = [*outs, ((8, 128), F32)] if token else outs
    operands = [v if isinstance(v, tuple) else (v, ENTIRE) for v in operands]

    def run(*refs):
        used = len(first) + len(operands)
        if token:
            *refs, done_ref = refs
            done_ref[...] = jnp.zeros_like(done_ref)
        kernel(*refs[:used], *refs[used + len(others) :])

    return pl.pallas_call(
        run,
        grid=(1,),
        in_specs=[SCALARS] * len(first) + [spec for _, spec in operands] + [ANYWHERE] * len(others),
        out_specs=[ENTIRE] * len(outs),
        out_shape=[
            (pltpu.HBM if math.prod(shape) * (2 if dtype == F32 else 1) > large else jax.ShapeDtypeStruct)(
                shape, dtype
            )
            for shape, dtype in outs
        ],
        compiler_params=pltpu.CompilerParams(vmem_limit_bytes=24 << 20),
        cost_estimate=pl.CostEstimate(flops=0, bytes_accessed=4 << 20, transcendentals=0),
    )(*first, *(v for v, _ in operands), *others)


def block_of(array, index):
    return array, pl.BlockSpec((128, 2048), lambda _: (index, 0))


def gate_kernel(*refs):
    pass


def joined(values, *others):
    return pl.pallas_call(
        gate_kernel,
        in_specs=[ANYWHERE] * (len(values) + len(others)),
        out_specs=[ANYWHERE] * len(values),
        out_shape=[pltpu.HBM(v.shape, v.dtype) for v in values],
        input_output_aliases={i: i for i in range(len(values))},
        cost_estimate=pl.CostEstimate(flops=0, bytes_accessed=0, transcendentals=0),
    )(*values, *others)


def split_kernel(one_ref, three_ref, low_ref, high_ref):
    half = low_ref.shape[0]
    low_ref[...] = three_ref[:half]
    high_ref[...] = one_ref[half:]


def pile_kernel(*refs):
    *pieces, out_ref = refs
    at = 0
    for piece in pieces:
        rows = piece.shape[0]
        out_ref[at : at + rows] = piece[...]
        at += rows


def gather_start(v):
    return swap_x(v, 1), swap_x(v, 3)


def gather_split(came, *others):
    rows, width = came[0].shape
    return small_call(split_kernel, [((rows // 2, width), BF16)] * 2, came, *others)


def gather_onward(onward):
    return swap_x(onward[0], 1), swap_x(onward[1], 3)


def gather_finish(v, came, opposite, *others):
    rows, width = v.shape
    pieces = [v, came[0], *opposite, came[1]]
    (own,) = small_call(pile_kernel, [((4 * rows, width), BF16)], pieces, *others)
    return own, swap_c(own)


def gather_group(v):
    came = gather_start(v)
    return gather_finish(v, came, gather_onward(gather_split(came)))


def add_low(*values):
    return sum(v.astype(F32) for v in values).astype(BF16)


def swap_cores(far):
    near, beyond = far
    return swap_c(beyond), swap_c(near)


def ring_two_kernel(own, beyond, low_ref, high_ref):
    two = add_low(own[...], beyond[...])
    half = low_ref.shape[0]
    low_ref[...] = two[:half]
    high_ref[...] = two[half:]


def ring_two(sums, *others):
    own, _, beyond = sums
    outs = [((64, 2048), BF16)] * 2
    ins = [part(own, (128, 2048), 2, 0), block_of(beyond, 0)]
    low, high, done = small_call(ring_two_kernel, outs, ins, *others, token=True)
    return (swap_x(low, 1), swap_x(high, 3)), done


def ring_next_kernel(own1, own3, near, beyond, add3_ref, add1_ref, s1_ref, s3_ref):
    half = add3_ref.shape[0]
    s3_ref[:half] = add_low(own3[:half], beyond[:half], add3_ref[...])
    s3_ref[half:] = add_low(own3[half:], beyond[half:])
    s1_ref[:half] = add_low(own1[:half], near[:half])
    s1_ref[half:] = add_low(own1[half:], near[half:], add1_ref[...])


def ring_next(sums, came, *others, large=2**18):
    own, near, beyond = sums
    own1, own3 = part(own, (128, 2048), 1, 0), part(own, (128, 2048), 3, 0)
    ins = [own1, own3, block_of(near, 1), block_of(beyond, 1), *came]
    return small_call(
        ring_next_kernel, [((128, 2048), BF16)] * 2, ins, *others, token=True, large=large
    )


def ring_last(sent):
    return swap_x(sent[0], 1), swap_x(sent[1], 3)


def axis_swap(v, axis, mask):
    return lax.ppermute(v, axis, [(i, i ^ mask) for i in range(4)])


def axis_next_kernel(a1, a3, add3_a, add1_a, b1, b3, add3_b, add1_b, *outs):
    for (one, three, add3, add1), (one_ref, three_ref) in (
        ((a1, a3, add3_a, add1_a), outs[:2]),
        ((b1, b3, add3_b, add1_b), outs[2:]),
    ):
        half = add3.shape[0]
        three_ref[:half] = add_low(three[0, :half], add3[...])
        three_ref[half:] = three[0, half:]
        one_ref[:half] = one[0, :half]
        one_ref[half:] = add_low(one[0, half:], add1[...])


def axis_next(axes, blocks, came, *others):
    a, b = blocks
    outs = [((a.shape[1], 512), BF16)] * 2 + [((b.shape[1], 512), BF16)] * 2
    pick = lambda v, i: part(v, (1, *v.shape[1:]), i, 0, 0)
    ins = [pick(a, 1), pick(a, 3), *came[:2], pick(b, 1), pick(b, 3), *came[2:]]
    one_a, three_a, one_b, three_b = small_call(axis_next_kernel, outs, ins, *others)
    return (
        axis_swap(one_a, axes[0], 1),
        axis_swap(three_a, axes[0], 3),
        axis_swap(one_b, axes[1], 1),
        axis_swap(three_b, axes[1], 3),
    )


def axis_turn_kernel(a_ref, a1, a3, b_ref, b1, b3, *outs):
    sum_a = add_low(a_ref[0], a1[...], a3[...]).reshape(4, 144, 512)
    sum_b = add_low(b_ref[0], b1[...], b3[...]).reshape(4, 128, 512)
    for i in range(4):
        outs[i][...] = sum_a[i]
        outs[4 + i][...] = sum_b[i]


def axis_turn(a, b, came, *others):
    ins = [part(a, (1, 576, 512), 0, 0, 0), *came[:2], part(b, (1, 512, 512), 0, 0, 0), *came[2:]]
    outs = [((144, 512), BF16)] * 4 + [((128, 512), BF16)] * 4
    own = small_call(axis_turn_kernel, outs, ins, *others)
    sum_a, sum_b = own[:4], own[4:]
    terms_a = [sum_a[0], *(axis_swap(sum_a[i], "y", i) for i in (2, 1, 3))]
    terms_b = [sum_b[0], *(axis_swap(sum_b[i], "z", i) for i in (2, 1, 3))]
    return terms_a, terms_b


def exchange(own, near, far, cross):
    return (
        own,
        swap_c(near),
        lax.ppermute(far, "xh", [(0, 1), (1, 0)]),
        lax.ppermute(cross, ("xh", "c"), [(i, 3 - i) for i in range(4)]),
    )


def spread_kernel(me_ref, *refs):
    parts, outs = refs[:-4], refs[-4:]
    for other, out_ref in enumerate(outs):
        quarter = me_ref[0] ^ other
        at = 0
        for part_ref in parts:
            if part_ref.shape[0] == 32:
                width = part_ref.shape[1] // 4
                start = pl.multiple_of(quarter * width, 128)
                out_ref[:32, at : at + width] = part_ref[:, pl.ds(start, width)]
                at += width
            else:
                out_ref[32:] = part_ref[...]


def collect_kernel(me_ref, *refs):
    *came, out_ref = refs
    for other, part_ref in enumerate(came):
        start = pl.multiple_of((me_ref[0] ^ other) * 32, 32)
        out_ref[pl.ds(start, 32)] = part_ref[:32]
    if out_ref.shape[0] > 128:
        out_ref[128:] = add_low(*(part_ref[32:] for part_ref in came))


def spread_columns(me, parts, *others, extra=None):
    below = 0 if extra is None else 16
    width = sum(p.shape[1] for p in parts) // 4
    ins = far(*parts) if extra is None else [*far(*parts), extra]
    sent = small_call(spread_kernel, [((32 + below, width), BF16)] * 4, ins, *others, scalars=me)
    (rows,) = small_call(
        collect_kernel, [((128 + below, width), BF16)], exchange(*sent), scalars=me
    )
    return rows


def rows_kernel(me_ref, rows_ref, *outs):
    for other, out_ref in enumerate(outs):
        start = pl.multiple_of((me_ref[0] ^ other) * 32, 32)
        out_ref[...] = rows_ref[pl.ds(start, 32)]


def return_kernel(me_ref, *refs):
    terms, outs = refs[:8], refs[8:]
    sum_a = add_low(*(v[...] for v in terms[:4]))
    sum_b = add_low(*(v[...] for v in terms[4:]))
    for at in range(4):
        rows = slice(at * 32, at * 32 + 32)

        for other, out_ref in enumerate(outs):

            @pl.when(me_ref[0] ^ other == at)
            def _():
                out_ref[:32, :512] = sum_a[rows]
                out_ref[:32, 512:] = sum_b[rows]

    for out_ref in outs:
        out_ref[32:, :512] = sum_a[128:]
        out_ref[32:, 512:] = jnp.zeros((16, 512), BF16)


def place_kernel(widths, me_ref, *refs):
    came, outs = refs[:4], refs[4:]
    for other, part_ref in enumerate(came):
        quarter = me_ref[0] ^ other
        at = 0
        for ref, width in zip(outs, widths):
            start = pl.multiple_of(quarter * width, 128)
            ref[:, pl.ds(start, width)] = part_ref[:32, at : at + width].astype(F32)
            at += width
    if len(outs) > len(widths):
        outs[-1][...] = sum(part_ref[32:, :256].astype(F32) for part_ref in came)


def two_pieces(v):
    high = lax.reduce_precision(v, 8, 7)
    return jnp.stack([high, v - high]).astype(BF16)


def small_block(vectors, joined_bias, unit_bias, starts, xh, c, t):
    flat = jnp.concatenate([*vectors, joined_bias, unit_bias])
    other = swap_x(flat, 1)
    pair = jnp.where(t == 0, jnp.stack([flat, other]), jnp.stack([other, flat]))
    pieces = two_pieces(pair)
    mine = (jnp.arange(4) == xh * 2 + c).astype(BF16)
    rows = pieces[:, :, :96].reshape(2, 2, 6, 16).transpose(2, 0, 1, 3).reshape(6, 2, 1, 32)
    rows = (rows * mine[:, None]).reshape(6, 256)
    joined = (pieces[:, :, 96:144].reshape(2, 1, 96) * mine[:, None]).reshape(2, 384)
    unit = (pieces[:, :, 144:].reshape(2, 1, 128) * mine[:, None]).reshape(2, 512)
    starts = (starts.astype(BF16) * mine[:, None]).reshape(1, 8)
    wide = lambda v: jnp.pad(v, ((0, 0), (0, 1024 - v.shape[1])))
    return jnp.concatenate(
        [wide(rows), wide(joined), wide(unit), wide(starts), jnp.zeros((5, 1024), BF16)], axis=0
    )


def low_half(rows):
    return lax.broadcasted_iota(jnp.int32, (rows, 128), 1) < 64


def store_plane(ref, values):
    low = low_half(values.shape[0])
    for j in range(8):
        a = values[:, j * 128 : j * 128 + 128]
        b = values[:, 1024 + j * 128 : 1024 + j * 128 + 128]
        at = j * 256
        ref[:, at : at + 128] = jnp.where(low, a, pltpu.roll(b, 64, 1)).astype(ref.dtype)
        ref[:, at + 128 : at + 256] = jnp.where(low, pltpu.roll(a, 64, 1), b).astype(ref.dtype)


def natural(values):
    low = low_half(values.shape[0])
    first, second = [], []
    for j in range(8):
        a = values[:, j * 256 : j * 256 + 128]
        b = values[:, j * 256 + 128 : j * 256 + 256]
        first.append(jnp.where(low, a, pltpu.roll(b, 64, 1)))
        second.append(jnp.where(low, pltpu.roll(a, 64, 1), b))
    return jnp.concatenate(first + second, axis=1)


def total_of(refs):
    return natural(sum(r[...].astype(F32) for r in refs))


def row_stats(values):
    centre = values - jnp.mean(values, axis=-1, keepdims=True)
    spread = jnp.mean(centre * centre, axis=-1, keepdims=True)
    return centre, lax.rsqrt(spread + EPS)


def norm_back(values, gain, upstream):
    centre, scale = row_stats(values)
    vhat = centre * scale
    e = upstream * gain
    dv = scale * (
        e - jnp.mean(e, axis=-1, keepdims=True) - vhat * jnp.mean(e * vhat, axis=-1, keepdims=True)
    )
    return dv, vhat


def first_norm_kernel(x_ref, *outs):
    n_ref, done_ref = outs[-2:]
    done_ref[...] = jnp.zeros_like(done_ref)
    centre, scale = row_stats(x_ref[...].astype(F32))
    store_plane(n_ref, centre * scale)


def middle_kernel(t0, t1, t2, t3, x_ref, small_ref, mid_ref, n_ref):
    small = natural(small_ref[...])
    middle = x_ref[...].astype(F32) + (total_of((t0, t1, t2, t3)) + small[2:3])
    mid_ref[...] = middle
    centre, scale = row_stats(middle)
    store_plane(n_ref, centre * scale * small[3:4] + small[4:5])


def second_back_kernel(
    t0, t1, t2, t3, mid_ref, cot_ref, small_ref, _, dh_ref, low_ref, sum_ref, part_ref
):
    small = natural(small_ref[...])
    upstream = total_of((t0, t1, t2, t3))
    dv, vhat = norm_back(mid_ref[...], small[3:4], upstream)
    final = cot_ref[...].astype(F32)
    dh = final + dv
    dh_ref[...] = dh
    store_plane(low_ref, dh)
    total = lambda v: jnp.sum(v, axis=0, keepdims=True)
    sums = [total(dh), total(upstream * vhat), total(upstream), total(final)]
    store_plane(part_ref, jnp.concatenate([*sums, jnp.zeros((4, 2048), F32)], axis=0))

    @pl.when(pl.program_id(0) == 0)
    def _():
        sum_ref[...] = jnp.zeros_like(sum_ref)

    sum_ref[...] += part_ref[...]


def first_back_kernel(t0, t1, t2, t3, x_ref, dh_ref, small_ref, g_ref):
    small = natural(small_ref[...])
    dv, _ = norm_back(x_ref[...].astype(F32), small[0:1], total_of((t0, t1, t2, t3)))
    g_ref[...] = dh_ref[...] + dv


def output_kernel(t0, t1, t2, t3, mid_ref, small_ref, o_ref):
    small = natural(small_ref[...])
    o_ref[...] = (mid_ref[...] + (total_of((t0, t1, t2, t3)) + small[5:6])).astype(BF16)


def plane_kernel(x_ref, o_ref):
    store_plane(o_ref, x_ref[...].astype(F32))


HALF_ROWS = pl.BlockSpec((64, 2048), lambda i: (i, 0))
PARAMS = pltpu.CompilerParams(vmem_limit_bytes=48 << 20)


def cost(flops, mebibytes):
    return pl.CostEstimate(flops=int(flops), bytes_accessed=int(mebibytes * 2**20), transcendentals=0)


def whole_call(kernel, outs, *operands):
    return pl.pallas_call(
        kernel, out_shape=outs, compiler_params=PARAMS, cost_estimate=cost(0, 4)
    )(*operands)


def row_block(width):
    return pl.BlockSpec((256, width), lambda i: (i, 0))


def whole(*shape):
    return pl.BlockSpec(shape, lambda i: (0,) * len(shape))


def halves(*block):
    tail = (0,) * (len(block) - 1)
    return [
        pl.BlockSpec(block, lambda i: (jnp.minimum(i, 1), *tail)),
        pl.BlockSpec(block, lambda i: (jnp.maximum(i - 2, 0), *tail)),
    ]


def pick(own_ref, other_ref):
    return jnp.where(pl.program_id(0) < 2, own_ref[...], other_ref[...])


def contract_both(own, other, right):
    half = right.shape[0] // 2
    return contract_rows(own, right[:half]) + contract_rows(other, right[half:])


def like(rows, dtype):
    return jax.ShapeDtypeStruct((rows, 2048), dtype)


def first_norm(x, half=None):
    at = 0 if half is None else 2
    return pl.pallas_call(
        first_norm_kernel,
        grid=(2,),
        in_specs=[row_block(2048)] + [ANYWHERE] * (half is not None),
        out_specs=[pl.BlockSpec((256, 2048), lambda i: (i + at, 0)), whole(8, 128)],
        out_shape=[pltpu.HBM((1024, 2048), F32), jax.ShapeDtypeStruct((8, 128), F32)],
        input_output_aliases={} if half is None else {1: 0},
        compiler_params=PARAMS,
        cost_estimate=cost(0, 8),
    )(*far(x), *(() if half is None else (half,)))


def up_grads_kernel(own_ref, other_ref, du_ref, out_ref, done_ref):
    done_ref[...] = jnp.zeros_like(done_ref)
    out_ref[...] = contract_both(own_ref[...], other_ref[...], du_ref[...]).astype(BF16)


def down_grads_kernel(_, own_ref, other_ref, a_ref, out_ref, done_ref):
    done_ref[...] = jnp.zeros_like(done_ref)
    out_ref[...] = contract_both(own_ref[...], other_ref[...], a_ref[...]).astype(BF16)


def up_grads(n, du):
    rows, width = du.shape
    return pl.pallas_call(
        up_grads_kernel,
        grid=(4,),
        in_specs=[pl.BlockSpec((512, 512), lambda i: (0, i))] * 2 + [whole(rows, width)],
        out_specs=[pl.BlockSpec((512, width), lambda i: (i, 0)), whole(8, 128)],
        out_shape=[
            pltpu.HBM((2048, 2 * width), BF16),
            jax.ShapeDtypeStruct((8, 128), F32),
        ],
        compiler_params=PARAMS,
        cost_estimate=cost(5e9, 10),
    )(*far(n[0]), n[1], *far(du))


def down_grads(left, cot, a):
    rows, width = a.shape
    return pl.pallas_call(
        down_grads_kernel,
        grid=(4,),
        in_specs=[ANYWHERE]
        + [pl.BlockSpec((512, 512), lambda i: (0, i))] * 2
        + [whole(rows, width)],
        out_specs=[pl.BlockSpec((512, width), lambda i: (i, 1)), whole(8, 128)],
        out_shape=[
            pltpu.HBM(left.shape, BF16),
            jax.ShapeDtypeStruct((8, 128), F32),
        ],
        input_output_aliases={0: 0},
        compiler_params=PARAMS,
        cost_estimate=cost(5e9, 10),
    )(left, *far(*cot, a))


def first_grads_kernel(
    place_ref, n_ref, own_ref, other_ref, df_ref, o_ref, w_ref, total_ref, unit_ref, small_ref, sums_ref,
    a_ref, b_ref, al_ref, ah_ref, bl_ref, bh_ref, done_ref
):
    done_ref[...] = jnp.zeros_like(done_ref)
    y = place_ref[1]
    joined = contract_rows(n_ref[...], df_ref[...])
    weight = w_ref[...].reshape(512, 768)
    weighted = joined * weight.astype(F32)
    weighted = sum(weighted[:, j * 128 : j * 128 + 128] for j in range(6))
    ones = jnp.ones((8, 128), BF16)
    high = weighted.astype(BF16)
    weighted = contract_cols(ones, high) + contract_cols(ones, (weighted - high.astype(F32)).astype(BF16))
    shift = contract_cols(total_ref[...].astype(BF16), weight)[0:1]
    gain = (weighted[0:1] - small_ref[1:2] * shift) / small_ref[0:1]
    sums = jnp.concatenate([sums_ref[:4], gain, shift, jnp.zeros((2, 512), F32)], axis=0)
    z = pl.program_id(0)
    z_to = z ^ place_ref[0]
    here = (z == place_ref[2]).astype(F32)
    row = lax.broadcasted_iota(jnp.int32, (8, 256), 0)
    row_of = lambda v, at: jnp.where(row == at, v[0:1, :256] * here, 0.0)
    joined_total = total_ref[...]
    joined = joined.astype(BF16)
    out = contract_both(own_ref[...], other_ref[...], o_ref[...]).astype(BF16)
    for i in range(4):
        rows = slice(i * 128, i * 128 + 128)
        mine = pltpu.roll(joined_total, 768 - i * 192, 1) if i else joined_total
        biases = row_of(mine, place_ref[3]) + row_of(
            unit_ref[:, i * 256 : i * 256 + 256], 2 + place_ref[3]
        )
        low = jnp.concatenate([sums[:, rows], jnp.zeros((8, 384), F32)], axis=1)
        high = jnp.concatenate([biases, jnp.zeros((8, 256), F32)], axis=1)
        below = jnp.concatenate([low, high], axis=0).astype(BF16)
        y_to = i ^ y
        a_ref[0, y_to, :128] = joined[rows, :512]
        a_ref[0, y_to, 128:] = below
        b_ref[y_to, 0, :, :256] = joined[rows, 512:]
        b_ref[y_to, 0, :, 256:] = out[rows]

        for half, (low_ref, high_ref) in enumerate(((al_ref, bl_ref), (ah_ref, bh_ref))):

            @pl.when((z_to == 2) & (y_to // 2 == half))
            def _():
                at = pl.multiple_of((y_to % 2) * 144, 16)
                low_ref[pl.ds(at, 128)] = joined[rows, :512]
                low_ref[pl.ds(at + 128, 16)] = below

            @pl.when((y_to == 2) & (z_to // 2 == half))
            def _():
                at = pl.multiple_of((z_to % 2) * 128, 128)
                high_ref[pl.ds(at, 128), :256] = joined[rows, 512:]
                high_ref[pl.ds(at, 128), 256:] = out[rows]


def first_grads_of(place, n, dh, df, o, first_all, total, unit_total, small, sums):
    rows = n.shape[0]
    return pl.pallas_call(
        first_grads_kernel,
        grid_spec=pltpu.PrefetchScalarGridSpec(
            num_scalar_prefetch=1,
            grid=(4,),
            in_specs=[
                pl.BlockSpec((rows, 512), lambda i, p: (0, i)),
                pl.BlockSpec((512, 512), lambda i, p: (0, i)),
                pl.BlockSpec((512, 512), lambda i, p: (0, i)),
                pl.BlockSpec((rows, 768), lambda i, p: (0, 0)),
                pl.BlockSpec((rows, 256), lambda i, p: (0, 0)),
                pl.BlockSpec((4, 128, 768), lambda i, p: (i, 0, 0)),
                pl.BlockSpec((8, 768), lambda i, p: (0, 0)),
                pl.BlockSpec((8, 1024), lambda i, p: (0, 0)),
                pl.BlockSpec((8, 512), lambda i, p: (0, i)),
                pl.BlockSpec((8, 512), lambda i, p: (0, i)),
            ],
            out_specs=[
                pl.BlockSpec((1, 4, 144, 512), lambda i, p: (i ^ p[0], 0, 0, 0)),
                pl.BlockSpec((4, 1, 128, 512), lambda i, p: (0, i ^ p[0], 0, 0)),
                *(pl.BlockSpec((v, 512), lambda i, p: (0, 0)) for v in (288, 288, 256, 256)),
                pl.BlockSpec((8, 128), lambda i, p: (0, 0)),
            ],
        ),
        out_shape=[
            pltpu.HBM((4, 4, 144, 512), BF16),
            pltpu.HBM((4, 4, 128, 512), BF16),
            *(jax.ShapeDtypeStruct((v, 512), BF16) for v in (288, 288, 256, 256)),
            jax.ShapeDtypeStruct((8, 128), F32),
        ],
        compiler_params=PARAMS,
        cost_estimate=cost(40e9, 16),
    )(place, *far(n, *dh, df, o, first_all), total, unit_total, small, sums)


def bias_of(info_ref, seq):
    flip_half = info_ref[8]
    row = lax.broadcasted_iota(jnp.int32, (256, 1), 0) ^ (flip_half * 128)
    col = lax.broadcasted_iota(jnp.int32, (1, 256), 1) ^ (flip_half * 128)
    allowed = col <= row
    place = (info_ref[9] ^ (seq % 2)) * 2 + (info_ref[10] ^ (seq // 2))
    for p in range(2):
        start = info_ref[place * 2 + p]
        in_row = (row >= start) & (row < start + PIECE)
        in_col = (col >= start) & (col < start + PIECE)
        allowed = allowed | (in_row & in_col)
    return jnp.abs(row - col).astype(F32), allowed


def softmax_of(slope, distance, allowed, query, keys):
    s = contract_cols(query, keys) * SCALE - slope * distance
    s = jnp.where(allowed, s, -1e30)
    e = jnp.exp(s - jnp.max(s, axis=-1, keepdims=True))
    return e * (1.0 / jnp.sum(e, axis=-1, keepdims=True))


def store_partial(out_refs, values):
    own_ref, near_ref, beyond_ref = out_refs
    step = pl.program_id(0)
    values = values.astype(BF16)

    @pl.when(step < 2)
    def _():
        own_ref[...] = values

    @pl.when(step == 2)
    def _():
        near_ref[...] = values

    @pl.when(step == 3)
    def _():
        beyond_ref[...] = values


PARTIAL_SPECS = [
    pl.BlockSpec((256, 2048), lambda i: (jnp.minimum(i, 1), 0)),
    pl.BlockSpec((256, 2048), lambda i: (0, 0)),
    pl.BlockSpec((256, 2048), lambda i: (0, 0)),
]
PARTIAL = [pltpu.HBM((rows, 2048), BF16) for rows in (512, 256, 256)]


def forward_kernel(
    info_ref, slopes_ref, v_ref, rows_ref, w_ref, _, n_ref, f_ref, o_ref, done_ref, small_ref, unit_ref,
    *out_refs
):
    seq = pl.program_id(0)
    *out_refs, bias_ref = out_refs

    @pl.when(seq == 0)
    def _():
        done_ref[...] = jnp.zeros_like(done_ref)
        for place in range(16):
            rows = rows_ref[place, :, :256].astype(F32)
            small_ref[:, place * 128 : place * 128 + 128] = (rows[:, :128] + rows[:, 128:])[:8]
        quarter, t = info_ref[9] * 2 + info_ref[10], info_ref[8]
        lane = lax.broadcasted_iota(jnp.int32, (1, 1024), 1)
        for first, width, ref in ((6, 192, bias_ref), (8, 256, unit_ref)):
            total = jnp.zeros((1, 1024), F32)
            for y in range(4):
                rows = rows_ref[quarter * 4 + y].astype(F32)
                rows = pltpu.roll(rows, (y * width - t * width + 1024) % 1024, 1)
                rows = rows[first : first + 1] + rows[first + 1 : first + 2]
                here = (lane >= y * width) & (lane < (y + 1) * width)
                total = total + jnp.where(here, rows, 0.0)
            ref[...] = jnp.broadcast_to(total[:, : ref.shape[1]], ref.shape)

    n = (v_ref[...] * small_ref[0:1] + small_ref[1:2]).astype(BF16)
    n_ref[...] = n
    weight = w_ref[...].reshape(2048, 1024)
    f = (jnp.dot(n, weight[:, :768], preferred_element_type=F32) + bias_ref[0:1]).astype(BF16)
    f_ref[...] = f
    distance, allowed = bias_of(info_ref, seq)
    mixed = []
    for head in range(2):
        q, k, v = (f[:, (head * 3 + i) * HD : (head * 3 + i + 1) * HD] for i in range(3))
        prob = softmax_of(slopes_ref[head], distance, allowed, q, k).astype(BF16)
        mixed.append(jnp.dot(prob, v, preferred_element_type=F32).astype(BF16))
    mixed = jnp.concatenate(mixed, axis=1)
    o_ref[...] = mixed
    store_partial(out_refs, contract_cols(mixed, weight[:, 768:]))


def backward_kernel(
    info_ref, slopes_ref, f_ref, own_ref, other_ref, w_ref, _, df_ref, sum_ref, *out_refs
):
    seq = pl.program_id(0)

    @pl.when(seq == 0)
    def _():
        sum_ref[...] = jnp.zeros_like(sum_ref)

    dh = pick(own_ref, other_ref)
    weight = w_ref[...].reshape(2048, 1024)
    grad = jnp.dot(
        dh, weight[:, 768:], preferred_element_type=F32
    ).astype(BF16)
    distance, allowed = bias_of(info_ref, seq)
    for head in range(2):
        base = head * 3 * HD
        q = f_ref[:, base : base + HD]
        k = f_ref[:, base + HD : base + 2 * HD]
        v = f_ref[:, base + 2 * HD : base + 3 * HD]
        g = grad[:, head * HD : (head + 1) * HD]
        prob = softmax_of(slopes_ref[head], distance, allowed, q, k)
        dp = contract_cols(g, v)
        row_dot = jnp.sum(prob * dp, axis=-1, keepdims=True)
        ds = (prob * (dp - row_dot) * SCALE).astype(BF16)
        dq = jnp.dot(ds, k, preferred_element_type=F32)
        dk = contract_rows(ds, q)
        dv = contract_rows(prob.astype(BF16), g)
        for i, part in enumerate((dq, dk, dv)):
            at = base + i * HD
            df_ref[:, at : at + HD] = part.astype(BF16)
            sum_ref[0:1, at : at + HD] += jnp.sum(part, axis=0, keepdims=True)
    store_partial(out_refs, contract_cols(df_ref[...], weight[:, :768]))


def forward_attention(info, slopes, vhat, first_all, other):
    rows = 1024
    return pl.pallas_call(
        forward_kernel,
        grid=(rows // 256,),
        in_specs=[
            SCALARS,
            SCALARS,
            row_block(2048),
            pl.BlockSpec((16, 16, 1024), lambda i: (0, 8, 0)),
            whole(16, 128, 1024),
            ANYWHERE,
        ],
        out_specs=[
            row_block(2048),
            row_block(768),
            row_block(256),
            whole(8, 128),
            whole(8, 2048),
            whole(8, 1024),
            *PARTIAL_SPECS,
        ],
        out_shape=[
            pltpu.HBM((rows, 2048), BF16),
            pltpu.HBM((rows, 768), BF16),
            pltpu.HBM((rows, 256), BF16),
            jax.ShapeDtypeStruct((8, 128), F32),
            like(8, F32),
            jax.ShapeDtypeStruct((8, 1024), F32),
            *PARTIAL,
        ],
        scratch_shapes=[pltpu.VMEM((8, 768), F32)],
        compiler_params=PARAMS,
        cost_estimate=cost(10e9, 24),
    )(info, slopes, *far(vhat, first_all, first_all), other)


def backward_attention(info, slopes, f, dh, first_all, other):
    rows = f.shape[0]
    return pl.pallas_call(
        backward_kernel,
        grid=(rows // 256,),
        in_specs=[
            SCALARS,
            SCALARS,
            row_block(768),
            *halves(256, 2048),
            whole(16, 128, 1024),
            ANYWHERE,
        ],
        out_specs=[row_block(768), whole(8, 768), *PARTIAL_SPECS],
        out_shape=[
            pltpu.HBM((rows, 768), BF16),
            jax.ShapeDtypeStruct((8, 768), F32),
            *PARTIAL,
        ],
        compiler_params=PARAMS,
        cost_estimate=cost(86e9, 10),
    )(info, slopes, *far(f, dh[0]), dh[1], *far(first_all), other)


def unit_kernel(n0_ref, n1_ref, c0_ref, c1_ref, w_ref, bias_ref, a_ref, du_ref, sum_ref, *out_refs):
    @pl.when(pl.program_id(0) == 0)
    def _():
        sum_ref[...] = jnp.zeros_like(sum_ref)

    n, cot = pick(n0_ref, n1_ref), pick(c0_ref, c1_ref)
    w_up, w_down = w_ref[:, :1024], w_ref[:, 1024:]
    u = jnp.dot(n, w_up, preferred_element_type=F32) + bias_ref[0:1]
    da = jnp.dot(cot, w_down, preferred_element_type=F32)
    a_ref[...] = gelu_tanh(u).astype(BF16)
    du = da * gelu_slope(u)
    sum_ref[0:1] += jnp.sum(du, axis=0, keepdims=True)
    du = du.astype(BF16)
    du_ref[...] = du
    total = contract_cols(du, w_up)
    store_partial(out_refs, total)


def units(n, cot, second_all, bias):
    rows = 1024
    return pl.pallas_call(
        unit_kernel,
        grid=(rows // 256,),
        in_specs=[
            *halves(256, 2048),
            *halves(256, 2048),
            whole(2048, 2048),
            whole(8, 1024),
        ],
        out_specs=[row_block(1024), row_block(1024), whole(8, 1024), *PARTIAL_SPECS],
        out_shape=[
            pltpu.HBM((rows, 1024), BF16),
            pltpu.HBM((rows, 1024), BF16),
            jax.ShapeDtypeStruct((8, 1024), F32),
            *PARTIAL,
        ],
        compiler_params=PARAMS,
        cost_estimate=cost(18e9, 24),
    )(*far(n[0]), n[1], *far(*cot, second_all), bias)


def unit_output_kernel(a_ref, w_ref, *out_refs):
    *out_refs, done_ref = out_refs
    done_ref[...] = jnp.zeros_like(done_ref)
    store_partial(out_refs, contract_cols(a_ref[...], w_ref[...]))


def unit_output(a, second_all):
    rows = a.shape[0]
    return pl.pallas_call(
        unit_output_kernel,
        grid=(rows // 256,),
        in_specs=[row_block(1024), pl.BlockSpec((2048, 1024), lambda i: (0, 1))],
        out_specs=[*PARTIAL_SPECS, whole(8, 128)],
        out_shape=[*PARTIAL, jax.ShapeDtypeStruct((8, 128), F32)],
        compiler_params=PARAMS,
        cost_estimate=cost(6e9, 12),
    )(*far(a, second_all))


def body(
    tokens,
    piece_starts,
    ln1_gain,
    ln1_bias,
    qkv_weight,
    qkv_bias,
    out_weight,
    out_bias,
    ln2_gain,
    ln2_bias,
    up_weight,
    up_bias,
    down_weight,
    down_bias,
    cotangent,
):
    xh, c, t = lax.axis_index("xh"), lax.axis_index("c"), lax.axis_index("t")
    quarter = xh * 2 + c

    me = quarter.reshape(1).astype(jnp.int32)
    small_own = small_block(
        (ln1_gain, ln1_bias, out_bias, ln2_gain, ln2_bias, down_bias), qkv_bias, up_bias, piece_starts, xh, c, t
    )
    first_rows = spread_columns(me, [qkv_weight, out_weight], extra=small_own)
    first_all = lax.all_gather(first_rows, PLANE, axis=0)
    second_rows = spread_columns(me, [up_weight, down_weight])
    second_all = lax.all_gather(second_rows, PLANE, axis=0, tiled=True)

    starts = first_rows[138, :8].astype(jnp.int32)
    info = jnp.concatenate([starts, jnp.stack([t, xh, c]).astype(jnp.int32)])
    head_ids = t * 8 + quarter * 2 + jnp.arange(2, dtype=jnp.int32)
    slopes = jnp.exp2(-8.0 * (head_ids.astype(F32) + 1.0) / H)

    came = gather_start(tokens)
    onward = gather_split(came, second_rows)
    tokens_all = gather_finish(tokens, came, gather_onward(onward))
    cot_plane = whole_call(plane_kernel, like(128, BF16), cotangent)
    came = gather_start(cot_plane)
    vhat, done = first_norm(tokens_all[1], first_norm(tokens_all[0])[0])
    onward = gather_split(came, done)
    opposite = gather_onward(onward)
    normed_all, f, mixed, done, small, bias_up, own, *other_core = forward_attention(
        info, slopes, vhat, first_all, onward[1]
    )
    cot_all = gather_finish(cot_plane, came, opposite, done)
    beyond, near = swap_cores(joined(other_core, cot_all[0]))
    sums = own, near, beyond
    from1, from3 = ring_last(ring_next(sums, ring_two(sums)[0]))
    middle, normed_two = pl.pallas_call(
        middle_kernel,
        grid=(2,),
        in_specs=[HALF_ROWS] * 5 + [whole(8, 2048)],
        out_specs=[HALF_ROWS] * 2,
        out_shape=[pltpu.HBM((128, 2048), F32), like(128, BF16)],
        compiler_params=PARAMS,
        cost_estimate=cost(0, 4),
    )(*far(own), near, from1, from3, tokens, small)
    normed_two_all = gather_group(normed_two)
    active, hidden_grad, unit_sums, own, *other_core = units(normed_two_all, cot_all, second_all, bias_up)

    beyond, near = swap_cores(other_core)
    sums = own, near, beyond
    came, _ = ring_two(sums)
    second_out, done = up_grads(normed_two_all, hidden_grad)
    from1, from3 = ring_last(ring_next(sums, came, done))
    second_out, done = down_grads(second_out, cot_all, active)
    second_grads = lax.psum_scatter(second_out, PLANE, scatter_dimension=0, tiled=True)
    middle_grad, branch_grad, row_sums = pl.pallas_call(
        second_back_kernel,
        grid=(2,),
        in_specs=[HALF_ROWS] * 6 + [whole(8, 2048), ANYWHERE],
        out_specs=[HALF_ROWS] * 2 + [whole(8, 2048)],
        out_shape=[pltpu.HBM((128, 2048), F32), like(128, BF16), like(8, F32)],
        scratch_shapes=[pltpu.VMEM((8, 2048), F32)],
        compiler_params=PARAMS,
        cost_estimate=cost(0, 4),
    )(*far(own), near, from1, from3, middle, cotangent, small, done)
    came = gather_start(branch_grad)
    out_own, *out_far, done = unit_output(active, second_all)
    onward = gather_split(came, done)
    branch_grad_all = gather_finish(branch_grad, came, gather_onward(onward))
    out_beyond, out_near = swap_cores(out_far)
    out_sums = out_own, out_near, out_beyond
    out_came, out_ready = ring_two(out_sums)

    joined_grad, joined_sums, one_own, *one_far = backward_attention(
        info, slopes, f, branch_grad_all, first_all, out_ready
    )
    out_sent = ring_next(out_sums, out_came, joined_sums, large=2**17)
    out_from1, out_from3 = ring_last(out_sent)
    one_beyond, one_near = swap_cores(joined(one_far, out_sent[1]))
    one_sums = one_own, one_near, one_beyond
    one_came, _ = ring_two(one_sums)
    place = jnp.stack([lax.axis_index("z"), lax.axis_index("y"), quarter, t]).astype(jnp.int32)
    grads_z, grads_y, *halves_of, done = first_grads_of(
        place, normed_all, branch_grad_all, joined_grad, mixed, first_all, joined_sums, unit_sums, small, row_sums
    )

    blocks = grads_z.reshape(4, 576, 512), grads_y.reshape(4, 512, 512)
    came = [
        axis_swap(v, axis, mask)
        for v, (axis, mask) in zip(halves_of, (("z", 1), ("z", 3), ("y", 1), ("y", 3)))
    ]
    sent = ring_next(one_sums, one_came, done, out_from1, out_from3)
    from1, from3 = ring_last(sent)
    came = axis_next(("z", "y"), blocks, came, sent[2])
    second_sent = small_call(rows_kernel, [((32, 2048), BF16)] * 4, [second_grads], scalars=me)
    second_came = exchange(*second_sent)
    grad_tokens, tokens_done = small_call(
        first_back_kernel,
        [((128, 2048), F32)],
        [part(one_own, (128, 2048), 0, 0), block_of(one_near, 0), from1, from3, tokens, middle_grad, small],
        token=True,
    )
    layer_out, out_done = small_call(
        output_kernel,
        [((128, 2048), BF16)],
        [part(out_own, (128, 2048), 0, 0), block_of(out_near, 0), out_from1, out_from3, middle, small],
        token=True,
    )

    terms_a, terms_b = axis_turn(*blocks, came, from1, from3, *second_came)
    first_sent = small_call(
        return_kernel,
        [((48, 1024), BF16)] * 4,
        [*terms_a, *terms_b],
        tokens_done,
        out_done,
        scalars=me,
    )

    grad_up, grad_down, place_done = small_call(
        functools.partial(place_kernel, (1024, 1024)),
        [((32, 4096), F32), ((32, 4096), F32)],
        second_came,
        scalars=me,
        token=True,
    )
    grad_qkv, grad_out, mine = small_call(
        functools.partial(place_kernel, (768, 256)),
        [((32, 3072), F32), ((32, 1024), F32), ((16, 256), F32)],
        exchange(*first_sent),
        place_done,
        scalars=me,
    )
    mine = mine + swap_x(mine, 1)
    vectors = lax.dynamic_slice(mine, (0, quarter * 32 + t * 16), (6, 16))
    joined_bias = lax.dynamic_slice(mine, (8 + xh, (c * 2 + t) * 48), (1, 48))
    unit_bias = lax.dynamic_slice(mine, (10 + xh, (c * 2 + t) * 64), (1, 64))

    return (
        layer_out,
        grad_tokens,
        vectors[4],
        vectors[5],
        grad_qkv,
        joined_bias[0],
        grad_out,
        vectors[0],
        vectors[1],
        vectors[2],
        grad_up,
        unit_bias[0],
        grad_down,
        vectors[3],
    )


def solution(mesh):
    fine = Mesh(mesh.devices.reshape(2, 4, 4, 2, 2), AXES)
    dp = ("xh", "z", "y", "c")
    rows, vec, mat = P(AXES, None), P(AXES), P(dp, "t")
    return jax.shard_map(
        body,
        mesh=fine,
        in_specs=(
            rows, P(dp, None), vec, vec, mat, vec, mat, vec, vec, vec, mat, vec, mat, vec, rows,
        ),
        out_specs=(
            rows, rows, vec, vec, mat, vec, mat, vec, vec, vec, mat, vec, mat, vec,
        ),
        check_vma=False,
    )
```
